128 devices in a mesh: pulse: 8 (over z_hi, x), gate: 16 (over y, z_lo, core).
Axes of the slice: x: 4, y: 4, z: 4 (z_hi: 2, z_lo: 2; z = z_hi * 2 + z_lo), core: 2. Of those that a mesh axis runs over, the one named last changes fastest.
Arguments:
- echoes: bfloat16 [2, 8, 2048, 4096], P(None, None, 'pulse', 'gate'), may hold values from -6 to 6
- replica: bfloat16 [2, 256], replicated, may hold values from -4 to 4
- beam_weights: float32 [2, 2, 8, 2048], P(None, None, None, 'pulse'), may hold values from -1.5 to 1.5
- track_doppler: int32 [32768], P(('pulse', 'gate')), may hold values from 0 to 2047, as said below
- track_gate: int32 [32768], P(('pulse', 'gate')), may hold values from 0 to 4095, as said below
- track_owner: int32 [32768], P(('pulse', 'gate')), may hold values from 0 to 127, as said below
Outputs:
- track_tiles: float32 [81920, 1024], P(('pulse', 'gate'))
The draws below stay inside these ranges and needn't reach their ends.
Inputs may be any that keep to these rules, and one draw needn't show every extreme that they name: `track_doppler`: row k lies in Doppler block (k // 256) // 16: its bin is in that block of 256 bins. `track_gate`: row k lies in range block (k // 256) % 16: its gate is in that block of 256 gates. `track_owner`: within each aligned block of 256 rows no owner appears more than 5 times, and in every draw some owner appears exactly 5 times in every block.
All inputs are finite; a program needn't handle non-finite values.
Results may differ from the reference program's by a relative error of at most 0.015.
Values may be sent and summed in bfloat16 or wider, within the bound.
A program may use at most 320 MiB of HBM per device.

```python
import math
import jax
import jax.numpy as jnp
from jax import lax

CH = 8
NPULSE = 2048
NGATE = 4096
CHIRP = 256
BEAMS = 2
TILE = 16
TRK_DEV = 256
DOP_DEV = 256
GATE_DEV = 256
RANGE_BLOCKS = 16
OWNERS = 128
CAP = 5
TRACKS = 32768


def draw_track_doppler(key, part):
    row_index = jnp.arange(TRACKS, dtype=jnp.int32)
    block_index = row_index // TRK_DEV // RANGE_BLOCKS
    offsets = jax.random.randint(jax.random.fold_in(key, 1), (TRACKS,), 0, DOP_DEV, dtype=jnp.int32)
    return block_index * DOP_DEV + offsets


def draw_track_gate(key, part):
    row_index = jnp.arange(TRACKS, dtype=jnp.int32)
    block_index = row_index // TRK_DEV % RANGE_BLOCKS
    offsets = jax.random.randint(jax.random.fold_in(key, 2), (TRACKS,), 0, GATE_DEV, dtype=jnp.int32)
    return block_index * GATE_DEV + offsets


def draw_track_owner(key, part):
    slot_total = OWNERS * CAP
    hot_owners = jax.random.permutation(jax.random.fold_in(key, 31), OWNERS)[:2]
    slot_owner = jnp.arange(slot_total, dtype=jnp.int32) // CAP
    is_hot = jnp.any(slot_owner[:, None] == hot_owners[None, :], axis=1)

    def one_block(holder):
        slot_order = jax.random.permutation(jax.random.fold_in(jax.random.fold_in(key, 37), holder), slot_total)
        cold_flag = jnp.where(is_hot[slot_order], 0, 1).astype(jnp.int32)
        chosen = slot_order[jnp.argsort(cold_flag, stable=True)][:TRK_DEV]
        shuffled = jax.random.permutation(jax.random.fold_in(jax.random.fold_in(key, 41), holder), chosen)
        return (shuffled // CAP).astype(jnp.int32)
    return jax.vmap(one_block)(jnp.arange(OWNERS, dtype=jnp.int32)).reshape(-1)


def level_of(own_key, extent, split, least, top_value):
    factor_of = 1.0
    for position, blocks in split:
        draws = jax.random.uniform(jax.random.fold_in(jax.random.fold_in(own_key, 6), position), (blocks,), jnp.float32, least / len(split), top_value / len(split))
        factor_of = factor_of * jnp.repeat(jnp.exp(draws), extent[position] // blocks).reshape((-1,) + (1,) * (len(extent) - 1 - position))
    return factor_of


def centred(own_key, shape, spread, reach, shards=(), kind=jnp.bfloat16):
    entries = spread * jax.random.normal(own_key, shape, jnp.float32)
    if shards:
        entries = entries * level_of(own_key, shape, shards, -0.22, 0.18)
    return jnp.clip(entries, -reach, reach).astype(kind)


def setup_inputs(seed: int = 0) -> dict:
    streams_of = jax.random.split(jax.random.key(seed), 7)
    return {
        "echoes": centred(streams_of[0], (2, CH, NPULSE, NGATE), 1.0, 6.0, ((2, 8), (3, 16))),
        "replica": centred(streams_of[1], (2, CHIRP), 1.0, 4.0),
        "beam_weights": centred(streams_of[2], (2, BEAMS, CH, NPULSE), (2 * CH) ** -0.5, 1.5, ((3, 8),), jnp.float32),
        "track_doppler": draw_track_doppler(jax.random.fold_in(streams_of[6], 71), 0),
        "track_gate": draw_track_gate(jax.random.fold_in(streams_of[6], 71), 0),
        "track_owner": draw_track_owner(jax.random.fold_in(streams_of[6], 71), 0),
    }


def reference(echoes, replica, beam_weights, track_doppler, track_gate, track_owner):
    range_scale = 1.0 / math.sqrt(2.0 * CHIRP)
    total_len = NGATE + CHIRP
    replica_wave = replica[0].astype(jnp.float32) + 1j * replica[1].astype(jnp.float32)
    replica_hat = jnp.conj(jnp.fft.fft(replica_wave, n=total_len))

    def one_channel(channel):
        echo_wave = channel[0].astype(jnp.float32) + 1j * channel[1].astype(jnp.float32)
        correlated = jnp.fft.ifft(jnp.fft.fft(echo_wave, n=total_len, axis=1) * replica_hat[None, :], axis=1)
        correlated = correlated[:, :NGATE] * range_scale
        comp_real = jnp.real(correlated).astype(jnp.bfloat16)
        comp_imag = jnp.imag(correlated).astype(jnp.bfloat16)
        comp_wave = comp_real.astype(jnp.float32) + 1j * comp_imag.astype(jnp.float32)
        spectral = jnp.fft.fft(comp_wave, axis=0) / math.sqrt(NPULSE)
        return jnp.stack([jnp.real(spectral).astype(jnp.bfloat16), jnp.imag(spectral).astype(jnp.bfloat16)])
    spectra = lax.map(one_channel, jnp.moveaxis(echoes, 1, 0))
    beam_real = jnp.zeros((BEAMS, NPULSE, NGATE), jnp.float32)
    beam_imag = jnp.zeros((BEAMS, NPULSE, NGATE), jnp.float32)
    for channel in range(CH):
        spec_real = spectra[channel, 0].astype(jnp.float32)[None]
        spec_imag = spectra[channel, 1].astype(jnp.float32)[None]
        weight_real = beam_weights[0, :, channel, :][:, :, None]
        weight_imag = beam_weights[1, :, channel, :][:, :, None]
        beam_real = beam_real + weight_real * spec_real - weight_imag * spec_imag
        beam_imag = beam_imag + weight_real * spec_imag + weight_imag * spec_real
    beams = jnp.stack([beam_real, beam_imag])
    half_tile = TILE // 2
    framed = jnp.pad(beams, ((0, 0), (0, 0), (half_tile, half_tile), (half_tile, half_tile)))
    zero_index = jnp.zeros((), jnp.int32)

    def cut_tile(doppler_bin, range_gate):
        starts = (zero_index, zero_index, doppler_bin.astype(jnp.int32), range_gate.astype(jnp.int32))
        return lax.dynamic_slice(framed, starts, (2, BEAMS, TILE, TILE)).reshape(-1)
    tile_rows = jax.vmap(cut_tile)(track_doppler.astype(jnp.int32), track_gate.astype(jnp.int32))
    owners = track_owner.astype(jnp.int32).reshape(OWNERS, TRK_DEV)
    owner_match = (owners[:, :, None] == jnp.arange(OWNERS, dtype=jnp.int32)[None, None, :]).astype(jnp.int32)
    running = jnp.cumsum(owner_match, axis=1, dtype=jnp.int32)
    slot_rank = (lax.optimization_barrier(jnp.sum(running * owner_match, axis=2, dtype=jnp.int32)) - 1).astype(jnp.int32)
    holder = jnp.broadcast_to(jnp.arange(OWNERS, dtype=jnp.int32)[:, None], owners.shape)
    row_index = ((owners * OWNERS + holder) * CAP + slot_rank).reshape(-1).astype(jnp.int32)
    result = jnp.zeros((OWNERS * OWNERS * CAP, tile_rows.shape[1]), jnp.float32)
    return result.at[row_index].set(tile_rows)
```

```python
import functools
import math

import jax
import jax.numpy as jnp
import numpy as np
from jax import lax
from jax.experimental import pallas as pl
from jax.experimental.pallas import tpu as pltpu
from jax.sharding import PartitionSpec as P

F32 = jnp.float32
BF16 = jnp.bfloat16
UNITS = 18
ROWS = 40
VMEM = pl.BlockSpec(memory_space=pltpu.VMEM)
SMEM = pl.BlockSpec(memory_space=pltpu.SMEM)


def tables():
    angle = 2.0 * np.pi * ((np.arange(256)[:, None] * np.arange(256)[None, :]) % 256) / 256.0
    cos, sin = np.cos(angle), np.sin(angle)
    dft = np.block([[cos, sin], [-sin, cos]]).astype(jnp.bfloat16)
    twist = 2.0 * np.pi * (np.arange(8)[:, None] * np.arange(256)[None, :]) / 2048.0
    scale = 1.0 / 1024.0
    return (
        dft,
        (np.cos(twist) * scale).astype(np.float32),
        (np.sin(twist) * scale).astype(np.float32),
    )


def cadd(a, b):
    return (a[0] + b[0], a[1] + b[1])


def csub(a, b):
    return (a[0] - b[0], a[1] - b[1])


def turn(a):
    return (a[1], -a[0])


def dft4(a):
    e0, e1 = cadd(a[0], a[2]), csub(a[0], a[2])
    f0, f1 = cadd(a[1], a[3]), turn(csub(a[1], a[3]))
    return [cadd(e0, f0), cadd(e1, f1), csub(e0, f0), csub(e1, f1)]


def dft8(x):
    root = math.sqrt(0.5)
    even = dft4([cadd(x[k], x[k + 4]) for k in range(4)])
    b = [csub(x[k], x[k + 4]) for k in range(4)]
    b1 = ((b[1][0] + b[1][1]) * root, (b[1][1] - b[1][0]) * root)
    b3 = ((b[3][1] - b[3][0]) * root, (b[3][0] + b[3][1]) * -root)
    odd = dft4([b[0], b1, turn(b[2]), b3])
    return [(even, odd)[d % 2][d // 2] for d in range(8)]


def doppler_channel(c, x_ref, w_ref, dft_ref, cos_ref, sin_ref, z_ref, acc_ref):
    for unit in range(2):
        for half in range(2):
            cols = slice(128 * half, 128 * half + 128)
            rows = slice(16 * unit, 16 * unit + 16)
            x = [
                tuple(x_ref[pb, q, c, rows, cols].astype(F32) for q in range(2)) for pb in range(8)
            ]
            for d, (re, im) in enumerate(dft8(x)):
                cos, sin = cos_ref[d : d + 1, cols], sin_ref[d : d + 1, cols]
                at = slice(128 * unit + 16 * d, 128 * unit + 16 * d + 16)
                z_ref[at, 128 * half : 128 * half + 128] = (re * cos + im * sin).astype(BF16)
                z_ref[at, 256 + 128 * half : 384 + 128 * half] = (im * cos - re * sin).astype(BF16)
    spec = lax.dot_general(
        dft_ref[...], z_ref[...], (((1,), (1,)), ((), ())), preferred_element_type=F32
    )
    lane = lax.broadcasted_iota(jnp.int32, (16, 16, 128), 2)
    keep = lane // 8 == lax.broadcasted_iota(jnp.int32, (16, 16, 128), 1)
    spread = (
        lax.broadcasted_iota(jnp.int32, (128, 128), 0) % 8
        == lax.broadcasted_iota(jnp.int32, (128, 128), 1) // 16
    )
    spread = jnp.where(spread, 1.0, 0.0).astype(BF16)
    for b in range(2):
        wide = []
        for q in range(2):
            w = jnp.where(keep, w_ref[(q * 2 + b) * 8 + c][:, None, :], 0.0).reshape(256, 128)
            high = w.astype(BF16)
            rest = w - high.astype(F32)
            mid = rest.astype(BF16)
            low = (rest - mid.astype(F32)).astype(BF16)
            wide.append(
                sum(jnp.dot(part, spread, preferred_element_type=F32) for part in (low, mid, high))
            )
        for unit in range(2):
            cols = slice(128 * unit, 128 * unit + 128)
            re, im = spec[:256, cols], spec[256:, cols]
            acc_ref[0, b, 8:264, cols] += wide[0] * re - wide[1] * im
            acc_ref[1, b, 8:264, cols] += wide[0] * im + wide[1] * re


def doppler_kernel(x_ref, w_ref, dft_ref, cos_ref, sin_ref, out_ref, z_ref, acc_ref):
    acc_ref[...] = jnp.zeros_like(acc_ref)

    def step(c, carry):
        doppler_channel(c, x_ref, w_ref, dft_ref, cos_ref, sin_ref, z_ref, acc_ref)
        return carry

    lax.fori_loop(0, 8, step, 0)
    for j in range(8):
        pack_block(j, acc_ref, out_ref)


def pack_block(j, acc_ref, out_ref):
    for unit in range(2):
        for q in range(2):
            both = jnp.concatenate(
                [
                    acc_ref[q, b, 32 * j + 7 : 32 * j + 7 + ROWS, 128 * unit : 128 * unit + 128]
                    for b in range(2)
                ],
                axis=0,
            )
            out_ref[j, unit, :, 128 * q : 128 * q + 128] = both.astype(BF16)


def taps_kernel(replica_ref, taps_ref):
    period = (
        lax.broadcasted_iota(jnp.int32, (16, 128), 0)
        == lax.broadcasted_iota(jnp.int32, (16, 128), 1) % 16
    )
    period = jnp.where(period, 1.0, 0.0).astype(F32)
    tables = []
    for q in range(2):
        row = jnp.concatenate(
            [replica_ref[q : q + 1, :].astype(F32), jnp.zeros((1, 128), F32)], axis=1
        )
        shifted = pltpu.roll(jnp.broadcast_to(row, (16, 384)), 0, 1, stride=1, stride_axis=0)
        tables.append(
            lax.dot_general(
                shifted.astype(BF16),
                period.astype(BF16),
                (((0,), (0,)), ((), ())),
                preferred_element_type=F32,
            )
        )
    lane = lax.broadcasted_iota(jnp.int32, (16, 128), 1) // 16
    for j in range(17):
        real, imag = (t[16 * j : 16 * j + 16] for t in tables)
        for d in range(8):
            keep = lane == d
            re, im = jnp.where(keep, real, 0.0), jnp.where(keep, imag, 0.0)
            from_real = jnp.concatenate([re, -im], axis=1).astype(BF16)
            from_imag = jnp.concatenate([im, re], axis=1).astype(BF16)
            taps_ref[j, 16 * d : 16 * d + 16, :] = from_real
            taps_ref[j, 128 + 16 * d : 144 + 16 * d, :] = from_imag


def compress(y_ref, taps_ref, sum_ref):
    depth = 2 * ROWS
    third = UNITS // 3

    def gates(block, first, count):
        x = jnp.concatenate(
            [
                y_ref[pl.ds(third * block + first + k, third)].reshape(third * depth, 256)
                for k in range(count)
            ],
            axis=1,
        )
        w = taps_ref[pl.ds(first, count)].reshape(256 * count, 256)
        return jnp.dot(x, w, preferred_element_type=F32)

    for block in range(3):
        rows = slice(block * third * depth, (block + 1) * third * depth)
        sum_ref[rows] = gates(block, 0, 5)
        for first in (5, 9, 13):
            sum_ref[rows] += gates(block, first, 4)


def frame(first_block, sum_ref, frame_ref):
    for unit in range(UNITS):
        for q in range(2):
            for b in range(2):
                for half in range(2):
                    start = (unit * 2 + b) * ROWS + half
                    value = sum_ref[start : start + 33, 128 * q : 128 * q + 128]
                    if unit == 0:
                        value = jnp.where(first_block, 0.0, value)
                    at = pl.ds(unit * 8 + q * 4 + b * 2 + half, 33, stride=8 * UNITS)
                    frame_ref[at, :] = value


def cut(base, shift, frame_ref):
    lane = lax.broadcasted_iota(jnp.int32, (8, 128), 1)
    gate = lane & 15
    gate_shift = shift & 15
    near_row, near_gate = lane >= shift - gate_shift, gate >= gate_shift
    f = [
        frame_ref[pl.ds(pl.multiple_of((base + step) * 8, 8), 8), :]
        for step in (0, 1, UNITS, UNITS + 1)
    ]
    z = jnp.where(
        near_row, jnp.where(near_gate, f[0], f[1]), jnp.where(near_gate, f[2], f[3])
    )
    return jnp.where(
        gate < 16 - gate_shift,
        pltpu.roll(z, (128 - shift) & 127, 1),
        pltpu.roll(z, (144 - shift) & 127, 1),
    )


def tiles_kernel(
    first_ref, base_ref, shift_ref, slot_ref, y_ref, taps_ref, out_ref, sum_ref, frame_ref, tile_ref
):
    compress(y_ref, taps_ref, sum_ref)
    frame(first_ref[0] > 0, sum_ref, frame_ref)
    tile_ref[...] = jnp.zeros_like(tile_ref)

    def step(k, carry):
        tile_ref[slot_ref[k]] = cut(base_ref[k], shift_ref[k], frame_ref)
        return carry

    lax.fori_loop(0, base_ref.shape[0], step, 0, unroll=8)
    out_ref[...] = tile_ref[...].reshape(out_ref.shape).astype(BF16)


def rows_kernel(in_ref, out_ref):
    slots = out_ref.shape[0]
    for k in range(8):
        out_ref[:, 128 * k : 128 * k + 128] = in_ref[pl.ds(k, slots, stride=8), :]


def shifted(value, steps):
    count = lax.axis_size("gate")
    pairs = [(i, i + steps) for i in range(count) if 0 <= i + steps < count]
    return lax.ppermute(value, "gate", pairs)


def params(mib, **more):
    return pltpu.CompilerParams(vmem_limit_bytes=mib << 20, **more)


def local(echoes, replica, beam_weights, track_doppler, track_gate, track_owner):
    pulse_devices, gate_devices = lax.axis_size("pulse"), lax.axis_size("gate")
    owners = pulse_devices * gate_devices
    tracks = track_owner.shape[0]
    capacity = 5
    dft, cos, sin = tables()

    strips = jnp.transpose(echoes, (3, 0, 1, 2)).reshape(8, 32, 2, 8, 256).transpose(0, 2, 3, 1, 4)
    gathered = lax.all_to_all(strips, "pulse", split_axis=0, concat_axis=0, tiled=True)
    weights = lax.all_gather(beam_weights, "pulse", axis=3, tiled=True).reshape(32, 16, 128)
    taps = pl.pallas_call(
        taps_kernel,
        out_shape=jax.ShapeDtypeStruct((17, 256, 256), BF16),
        in_specs=[VMEM],
        out_specs=VMEM,
        compiler_params=params(24),
        cost_estimate=pl.CostEstimate(flops=10**7, bytes_accessed=2**22, transcendentals=0),
    )(replica)

    blocks = pl.pallas_call(
        doppler_kernel,
        out_shape=jax.ShapeDtypeStruct((8, 2, 2 * ROWS, 256), BF16),
        in_specs=[VMEM] * 5,
        out_specs=VMEM,
        scratch_shapes=[pltpu.VMEM((256, 512), BF16), pltpu.VMEM((2, 2, 272, 256), F32)],
        compiler_params=params(24),
    )(gathered, weights, jnp.asarray(dft), jnp.asarray(cos), jnp.asarray(sin))
    own = lax.all_to_all(blocks, "pulse", split_axis=0, concat_axis=0, tiled=True).reshape(
        16, 2 * ROWS, 256
    )
    y = jnp.concatenate(
        [shifted(own[15:], 1), own, shifted(own, -1), shifted(own[:1], -2)], axis=0
    )

    row_in, gate_in = track_doppler % 256, track_gate % 256 + 8
    base = row_in // 8 * UNITS + gate_in // 16
    shift = row_in % 8 * 16 + gate_in % 16
    order = jnp.arange(tracks, dtype=jnp.int32)
    earlier = (track_owner[:, None] == track_owner[None, :]) & (order[None, :] < order[:, None])
    rank = jnp.sum(earlier.astype(jnp.int32), axis=1, dtype=jnp.int32)
    slot = track_owner * capacity + rank
    first = (lax.axis_index("gate") == 0).astype(jnp.int32).reshape(1)

    outgoing = pl.pallas_call(
        tiles_kernel,
        out_shape=jax.ShapeDtypeStruct((owners, capacity * 8, 128), BF16),
        in_specs=[SMEM] * 4 + [VMEM] * 2,
        out_specs=VMEM,
        scratch_shapes=[
            pltpu.VMEM((UNITS * 2 * ROWS, 256), F32),
            pltpu.VMEM((33 * UNITS * 8, 128), F32),
            pltpu.VMEM((owners * capacity, 8, 128), F32),
        ],
        compiler_params=params(32),
    )(first, base, shift, slot, y, taps)
    received = lax.all_to_all(
        outgoing, ("pulse", "gate"), split_axis=0, concat_axis=0, tiled=True
    )
    wide = received.reshape(owners * capacity * 8, 128).astype(F32)
    return pl.pallas_call(
        rows_kernel,
        out_shape=jax.ShapeDtypeStruct((owners * capacity, 1024), F32),
        in_specs=[VMEM],
        out_specs=VMEM,
        compiler_params=params(16),
    )(wide)


def solution(mesh):
    return jax.shard_map(
        local,
        mesh=mesh,
        in_specs=(
            P(None, None, "pulse", "gate"),
            P(),
            P(None, None, None, "pulse"),
            P(("pulse", "gate")),
            P(("pulse", "gate")),
            P(("pulse", "gate")),
        ),
        out_specs=P(("pulse", "gate"), None),
        check_vma=False,
    )
```

```python
import functools
import math

import jax
import jax.numpy as jnp
import numpy as np
from jax import lax
from jax.experimental import pallas as pl
from jax.experimental.pallas import tpu as pltpu
from jax.sharding import PartitionSpec as P

F32 = jnp.float32
BF16 = jnp.bfloat16
UNITS = 18
ROWS = 40
VMEM = pl.BlockSpec(memory_space=pltpu.VMEM)
SMEM = pl.BlockSpec(memory_space=pltpu.SMEM)


def tables():
    angle = 2.0 * np.pi * ((np.arange(256)[:, None] * np.arange(256)[None, :]) % 256) / 256.0
    cos, sin = np.cos(angle), np.sin(angle)
    dft = np.block([[cos, sin], [-sin, cos]]).astype(jnp.bfloat16)
    twist = 2.0 * np.pi * (np.arange(8)[:, None] * np.arange(256)[None, :]) / 2048.0
    scale = 1.0 / 1024.0
    return (
        dft,
        (np.cos(twist) * scale).astype(np.float32),
        (np.sin(twist) * scale).astype(np.float32),
    )


def cadd(a, b):
    return (a[0] + b[0], a[1] + b[1])


def csub(a, b):
    return (a[0] - b[0], a[1] - b[1])


def turn(a):
    return (a[1], -a[0])


def dft4(a):
    e0, e1 = cadd(a[0], a[2]), csub(a[0], a[2])
    f0, f1 = cadd(a[1], a[3]), turn(csub(a[1], a[3]))
    return [cadd(e0, f0), cadd(e1, f1), csub(e0, f0), csub(e1, f1)]


def dft8(x):
    root = math.sqrt(0.5)
    even = dft4([cadd(x[k], x[k + 4]) for k in range(4)])
    b = [csub(x[k], x[k + 4]) for k in range(4)]
    b1 = ((b[1][0] + b[1][1]) * root, (b[1][1] - b[1][0]) * root)
    b3 = ((b[3][1] - b[3][0]) * root, (b[3][0] + b[3][1]) * -root)
    odd = dft4([b[0], b1, turn(b[2]), b3])
    return [(even, odd)[d % 2][d // 2] for d in range(8)]


def doppler_channel(c, x_ref, wide_ref, dft_ref, cos_ref, sin_ref, z_ref, acc_ref):
    for unit in range(2):
        for half in range(2):
            cols = slice(128 * half, 128 * half + 128)
            rows = slice(16 * unit, 16 * unit + 16)
            x = [tuple(x_ref(pb, q)[rows, cols].astype(F32) for q in range(2)) for pb in range(8)]
            for d, (re, im) in enumerate(dft8(x)):
                cos, sin = cos_ref[d : d + 1, cols], sin_ref[d : d + 1, cols]
                at = slice(128 * unit + 16 * d, 128 * unit + 16 * d + 16)
                z_ref[at, 128 * half : 128 * half + 128] = (re * cos + im * sin).astype(BF16)
                z_ref[at, 256 + 128 * half : 384 + 128 * half] = (im * cos - re * sin).astype(BF16)
    spec = lax.dot_general(
        dft_ref[...], z_ref[...], (((1,), (1,)), ((), ())), preferred_element_type=F32
    )
    for b in range(2):
        real, imag = (wide_ref[(q * 2 + b) * 8 + c] for q in range(2))
        for unit in range(2):
            cols = slice(128 * unit, 128 * unit + 128)
            re, im = spec[:256, cols], spec[256:, cols]
            acc_ref[0, b, 8:264, cols] += real * re - imag * im
            acc_ref[1, b, 8:264, cols] += real * im + imag * re


def widen(i, weight_ref, wide_ref):
    lane = lax.broadcasted_iota(jnp.int32, (16, 128), 1)
    keep = lane // 8 == lax.broadcasted_iota(jnp.int32, (16, 128), 0)
    spread = (
        lax.broadcasted_iota(jnp.int32, (128, 128), 0) % 8
        == lax.broadcasted_iota(jnp.int32, (128, 128), 1) // 16
    )
    spread = jnp.where(spread, 1.0, 0.0).astype(BF16)
    w = jnp.concatenate(
        [
            jnp.where(keep, weight_ref[source, half, pl.ds(i, 1), :], 0.0)
            for source in range(8)
            for half in range(2)
        ],
        axis=0,
    )
    high = w.astype(BF16)
    rest = w - high.astype(F32)
    mid = rest.astype(BF16)
    low = (rest - mid.astype(F32)).astype(BF16)
    wide_ref[i] = sum(jnp.dot(part, spread, preferred_element_type=F32) for part in (low, mid, high))


def pack_block(j, acc_ref, out_ref):
    for unit in range(2):
        for q in range(2):
            both = jnp.concatenate(
                [
                    acc_ref[q, b, 32 * j + 7 : 32 * j + 7 + ROWS, 128 * unit : 128 * unit + 128]
                    for b in range(2)
                ],
                axis=0,
            )
            out_ref[unit, :, 128 * q : 128 * q + 128] = both.astype(BF16)


def make_taps(replica_ref, taps_ref):
    period = (
        lax.broadcasted_iota(jnp.int32, (16, 128), 0)
        == lax.broadcasted_iota(jnp.int32, (16, 128), 1) % 16
    )
    period = jnp.where(period, 1.0, 0.0).astype(F32)
    tables = []
    for q in range(2):
        row = jnp.concatenate(
            [replica_ref[q : q + 1, :].astype(F32), jnp.zeros((1, 128), F32)], axis=1
        )
        shifted = pltpu.roll(jnp.broadcast_to(row, (16, 384)), 0, 1, stride=1, stride_axis=0)
        tables.append(
            lax.dot_general(
                shifted.astype(BF16),
                period.astype(BF16),
                (((0,), (0,)), ((), ())),
                preferred_element_type=F32,
            )
        )
    lane = lax.broadcasted_iota(jnp.int32, (16, 128), 1) // 16
    for j in range(17):
        real, imag = (t[16 * j : 16 * j + 16] for t in tables)
        for d in range(8):
            keep = lane == d
            re, im = jnp.where(keep, real, 0.0), jnp.where(keep, imag, 0.0)
            from_real = jnp.concatenate([re, -im], axis=1).astype(BF16)
            from_imag = jnp.concatenate([im, re], axis=1).astype(BF16)
            taps_ref[j, 16 * d : 16 * d + 16, :] = from_real
            taps_ref[j, 128 + 16 * d : 144 + 16 * d, :] = from_imag


def compress(y_ref, taps_ref, sum_ref):
    depth = 2 * ROWS
    third = UNITS // 3

    def gates(block, first, count):
        x = jnp.concatenate(
            [
                y_ref[pl.ds(third * block + first + k, third)].reshape(third * depth, 256)
                for k in range(count)
            ],
            axis=1,
        )
        w = taps_ref[pl.ds(first, count)].reshape(256 * count, 256)
        return jnp.dot(x, w, preferred_element_type=F32)

    for block in range(3):
        rows = slice(block * third * depth, (block + 1) * third * depth)
        sum_ref[rows] = gates(block, 0, 5)
        for first in (5, 9, 13):
            sum_ref[rows] += gates(block, first, 4)


def frame(first_block, sum_ref, frame_ref):
    for unit in range(UNITS):
        for q in range(2):
            for b in range(2):
                for half in range(2):
                    start = (unit * 2 + b) * ROWS + half
                    value = sum_ref[start : start + 33, 128 * q : 128 * q + 128]
                    if unit == 0:
                        value = jnp.where(first_block, 0.0, value)
                    at = pl.ds(unit * 8 + q * 4 + b * 2 + half, 33, stride=8 * UNITS)
                    frame_ref[at, :] = value


def cut(base, shift, frame_ref):
    lane = lax.broadcasted_iota(jnp.int32, (8, 128), 1)
    gate = lane & 15
    gate_shift = shift & 15
    near_row, near_gate = lane >= shift - gate_shift, gate >= gate_shift
    f = [
        frame_ref[pl.ds(pl.multiple_of((base + step) * 8, 8), 8), :]
        for step in (0, 1, UNITS, UNITS + 1)
    ]
    z = jnp.where(
        near_row, jnp.where(near_gate, f[0], f[1]), jnp.where(near_gate, f[2], f[3])
    )
    return jnp.where(
        gate < 16 - gate_shift,
        pltpu.roll(z, (128 - shift) & 127, 1),
        pltpu.roll(z, (144 - shift) & 127, 1),
    )


CHUNKS = 4
PER = 8 // CHUNKS


def beams_kernel(
    echo_ref,
    weight_ref,
    replica_ref,
    dft_ref,
    cos_ref,
    sin_ref,
    frame_ref,
    out_strip,
    in_strip,
    all_weights,
    wide_ref,
    z_ref,
    acc_ref,
    out_block,
    y_ref,
    taps_ref,
    sum_ref,
    strip_sent,
    strip_here,
    strip_own,
    weight_sent,
    weight_here,
    block_sent,
    block_here,
    halo_sent,
    halo_here,
    edge_sent,
    edge_here,
):
    me, g = lax.axis_index("pulse"), lax.axis_index("gate")
    gates = lax.axis_size("gate")
    barrier = pltpu.get_barrier_semaphore()

    def at(pulse, gate):
        return dict(device_id=(pulse, gate), device_id_type=pl.DeviceIdType.MESH)

    def peer(k):
        return lax.rem(me + k, 8)

    for k in range(1, 8):
        pl.semaphore_signal(barrier, inc=1, **at(peer(k), g))
    near = jnp.int32(7)
    for step in (-2, -1, 1, 2):
        there = (g + step >= 0) & (g + step < gates)
        near += there.astype(jnp.int32)

        @pl.when(there)
        def _():
            pl.semaphore_signal(barrier, inc=1, **at(me, g + step))

    def strip(chunk, target, source):
        return pltpu.make_async_remote_copy(
            src_ref=out_strip.at[chunk, target],
            dst_ref=in_strip.at[chunk, source],
            send_sem=strip_sent.at[chunk, target],
            recv_sem=strip_here.at[chunk, source],
            **at(target, g),
        )

    def own_strip(chunk):
        return pltpu.make_async_copy(
            out_strip.at[chunk, me], in_strip.at[chunk, me], strip_own.at[chunk]
        )

    def weight(target, source):
        return pltpu.make_async_remote_copy(
            src_ref=weight_ref,
            dst_ref=all_weights.at[source],
            send_sem=weight_sent.at[target],
            recv_sem=weight_here.at[source],
            **at(target, g),
        )

    def block(target, source):
        return pltpu.make_async_remote_copy(
            src_ref=out_block.at[target],
            dst_ref=y_ref.at[pl.ds(1 + 2 * source, 2)],
            send_sem=block_sent.at[target],
            recv_sem=block_here.at[source],
            **at(target, g),
        )

    def halo(source):
        return pltpu.make_async_remote_copy(
            src_ref=y_ref.at[pl.ds(1 + 2 * source, 2)],
            dst_ref=y_ref.at[pl.ds(17 + 2 * source, 2)],
            send_sem=halo_sent.at[source],
            recv_sem=halo_here.at[source],
            **at(me, g - 1),
        )

    def edge(which):
        return pltpu.make_async_remote_copy(
            src_ref=y_ref.at[(1, 16)[which]],
            dst_ref=y_ref.at[(33, 0)[which]],
            send_sem=edge_sent.at[which],
            recv_sem=edge_here.at[which],
            **at(me, (g - 2, g + 1)[which]),
        )

    def turn_chunk(chunk):
        for c in range(PER):
            for q in range(2):
                turned = echo_ref[q, chunk * PER + c].T
                out_strip[chunk, :, q, c] = turned.reshape(8, 32, 256)

    def send_chunk(chunk):
        for k in range(1, 8):
            strip(chunk, peer(k), me).start()
        own_strip(chunk).start()

    turn_chunk(0)
    pl.semaphore_wait(barrier, near)
    send_chunk(0)
    for k in range(1, 8):
        weight(peer(k), me).start()

    def turn_and_send(chunk, carry):
        turn_chunk(chunk)
        send_chunk(chunk)
        return carry

    lax.fori_loop(1, CHUNKS, turn_and_send, 0)

    all_weights[me] = weight_ref[...]
    acc_ref[...] = jnp.zeros_like(acc_ref)
    nothing = jnp.zeros((2 * ROWS, 256), BF16)

    @pl.when(g == 0)
    def _():
        y_ref[0] = nothing

    @pl.when(g == gates - 1)
    def _():
        for unit in range(17, 33):
            y_ref[unit] = nothing

    @pl.when(g >= gates - 2)
    def _():
        y_ref[33] = nothing

    make_taps(replica_ref, taps_ref)
    for k in range(1, 8):
        weight(me, peer(k)).wait_recv()

    def widen_step(i, carry):
        widen(i, all_weights, wide_ref)
        return carry

    lax.fori_loop(0, 32, widen_step, 0)

    def doppler_chunk(chunk, carry):
        own_strip(chunk).wait()
        for k in range(1, 8):
            strip(chunk, me, peer(k)).wait_recv()

        def one(c, inner):
            doppler_channel(
                chunk * PER + c,
                lambda pb, q: in_strip.at[chunk, pb, q, c],
                wide_ref,
                dft_ref,
                cos_ref,
                sin_ref,
                z_ref,
                acc_ref,
            )
            return inner

        return lax.fori_loop(0, PER, one, carry)

    lax.fori_loop(0, CHUNKS, doppler_chunk, 0)

    for j in range(8):

        @pl.when(me == j)
        def _():
            pack_block(j, acc_ref, y_ref.at[pl.ds(1 + 2 * j, 2)])

        @pl.when(me != j)
        def _():
            pack_block(j, acc_ref, out_block.at[j])
            block(j, me).start()

    def pass_on(source):
        @pl.when(g > 0)
        def _():
            halo(source).start()

        @pl.when((source == 0) & (g > 1))
        def _():
            edge(0).start()

        @pl.when((source == 7) & (g < gates - 1))
        def _():
            edge(1).start()

    pass_on(me)

    def arrive(k, carry):
        source = lax.rem(me + k, 8)
        block(me, source).wait_recv()
        pass_on(source)
        return carry

    lax.fori_loop(1, 8, arrive, 0)

    @pl.when(g < gates - 1)
    def _():
        for source in range(8):
            halo(source).wait_recv()

    @pl.when(g < gates - 2)
    def _():
        edge(0).wait_recv()

    @pl.when(g > 0)
    def _():
        edge(1).wait_recv()

    compress(y_ref, taps_ref, sum_ref)
    frame(g == 0, sum_ref, frame_ref)

    @pl.when(g > 0)
    def _():
        for source in range(8):
            halo(source).wait_send()

    @pl.when(g > 1)
    def _():
        edge(0).wait_send()

    @pl.when(g < gates - 1)
    def _():
        edge(1).wait_send()

    for k in range(1, 8):
        weight(peer(k), me).wait_send()
        block(peer(k), me).wait_send()

    def sent(chunk, carry):
        for k in range(1, 8):
            strip(chunk, peer(k), me).wait_send()
        return carry

    lax.fori_loop(0, CHUNKS, sent, 0)


def beams(echoes, weights, replica):
    dft, cos, sin = tables()
    dma = pltpu.SemaphoreType.DMA
    return pl.pallas_call(
        beams_kernel,
        out_shape=jax.ShapeDtypeStruct((33 * UNITS * 8, 128), F32),
        in_specs=[VMEM] * 6,
        out_specs=VMEM,
        scratch_shapes=[
            pltpu.VMEM((CHUNKS, 8, 2, PER, 32, 256), BF16),
            pltpu.VMEM((CHUNKS, 8, 2, PER, 32, 256), BF16),
            pltpu.VMEM((8, 2, 32, 128), F32),
            pltpu.VMEM((32, 256, 128), F32),
            pltpu.VMEM((256, 512), BF16),
            pltpu.VMEM((2, 2, 272, 256), F32),
            pltpu.VMEM((8, 2, 2 * ROWS, 256), BF16),
            pltpu.VMEM((34, 2 * ROWS, 256), BF16),
            pltpu.VMEM((17, 256, 256), BF16),
            pltpu.VMEM((UNITS * 2 * ROWS, 256), F32),
            dma((CHUNKS, 8)),
            dma((CHUNKS, 8)),
            dma((CHUNKS,)),
            dma((8,)),
            dma((8,)),
            dma((8,)),
            dma((8,)),
            dma((8,)),
            dma((8,)),
            dma((2,)),
            dma((2,)),
        ],
        compiler_params=params(48, collective_id=0, has_side_effects=True),
        cost_estimate=pl.CostEstimate(flops=6 * 10**9, bytes_accessed=8 << 20, transcendentals=0),
    )(echoes, weights, replica, jnp.asarray(dft), jnp.asarray(cos), jnp.asarray(sin))


def tiles_kernel(base_ref, shift_ref, slot_ref, frame_ref, out_ref, tile_ref):
    tile_ref[...] = jnp.zeros_like(tile_ref)

    def step(k, carry):
        tile_ref[slot_ref[k]] = cut(base_ref[k], shift_ref[k], frame_ref)
        return carry

    lax.fori_loop(0, base_ref.shape[0], step, 0, unroll=8)
    out_ref[...] = tile_ref[...].reshape(out_ref.shape).astype(BF16)


def rows_kernel(in_ref, out_ref):
    slots = out_ref.shape[0]
    for k in range(8):
        out_ref[:, 128 * k : 128 * k + 128] = in_ref[pl.ds(k, slots, stride=8), :]


def params(mib, **more):
    return pltpu.CompilerParams(vmem_limit_bytes=mib << 20, **more)


def local(echoes, replica, beam_weights, track_doppler, track_gate, track_owner):
    pulse_devices, gate_devices = lax.axis_size("pulse"), lax.axis_size("gate")
    owners = pulse_devices * gate_devices
    tracks = track_owner.shape[0]
    capacity = 5
    weights = beam_weights.reshape(32, 2, 128).transpose(1, 0, 2)
    frames = beams(echoes, weights, replica)

    row_in, gate_in = track_doppler % 256, track_gate % 256 + 8
    base = row_in // 8 * UNITS + gate_in // 16
    shift = row_in % 8 * 16 + gate_in % 16
    order = jnp.arange(tracks, dtype=jnp.int32)
    earlier = (track_owner[:, None] == track_owner[None, :]) & (order[None, :] < order[:, None])
    rank = jnp.sum(earlier.astype(jnp.int32), axis=1, dtype=jnp.int32)
    slot = track_owner * capacity + rank

    outgoing = pl.pallas_call(
        tiles_kernel,
        out_shape=jax.ShapeDtypeStruct((owners, capacity * 8, 128), BF16),
        in_specs=[SMEM] * 3 + [VMEM],
        out_specs=VMEM,
        scratch_shapes=[pltpu.VMEM((owners * capacity, 8, 128), F32)],
        compiler_params=params(24),
    )(base, shift, slot, frames)
    received = lax.all_to_all(
        outgoing, ("pulse", "gate"), split_axis=0, concat_axis=0, tiled=True
    )
    wide = received.reshape(owners * capacity * 8, 128).astype(F32)
    return pl.pallas_call(
        rows_kernel,
        out_shape=jax.ShapeDtypeStruct((owners * capacity, 1024), F32),
        in_specs=[VMEM],
        out_specs=VMEM,
        compiler_params=params(16),
    )(wide)


def solution(mesh):
    return jax.shard_map(
        local,
        mesh=mesh,
        in_specs=(
            P(None, None, "pulse", "gate"),
            P(),
            P(None, None, None, "pulse"),
            P(("pulse", "gate")),
            P(("pulse", "gate")),
            P(("pulse", "gate")),
        ),
        out_specs=P(("pulse", "gate"), None),
        check_vma=False,
    )
```

```python
import functools
import math

import jax
import jax.numpy as jnp
import numpy as np
from jax import lax
from jax.experimental import pallas as pl
from jax.experimental.pallas import tpu as pltpu
from jax.sharding import PartitionSpec as P

F32 = jnp.float32
BF16 = jnp.bfloat16
UNITS = 18
ROWS = 40
VMEM = pl.BlockSpec(memory_space=pltpu.VMEM)
SMEM = pl.BlockSpec(memory_space=pltpu.SMEM)


def tables():
    angle = 2.0 * np.pi * ((np.arange(256)[:, None] * np.arange(256)[None, :]) % 256) / 256.0
    cos, sin = np.cos(angle), np.sin(angle)
    dft = np.block([[cos, sin], [-sin, cos]]).astype(jnp.bfloat16)
    twist = 2.0 * np.pi * (np.arange(8)[:, None] * np.arange(256)[None, :]) / 2048.0
    scale = 1.0 / 1024.0
    return (
        dft,
        (np.cos(twist) * scale).astype(np.float32),
        (np.sin(twist) * scale).astype(np.float32),
    )


def cadd(a, b):
    return (a[0] + b[0], a[1] + b[1])


def csub(a, b):
    return (a[0] - b[0], a[1] - b[1])


def turn(a):
    return (a[1], -a[0])


def dft4(a):
    e0, e1 = cadd(a[0], a[2]), csub(a[0], a[2])
    f0, f1 = cadd(a[1], a[3]), turn(csub(a[1], a[3]))
    return [cadd(e0, f0), cadd(e1, f1), csub(e0, f0), csub(e1, f1)]


def dft8(x):
    root = math.sqrt(0.5)
    even = dft4([cadd(x[k], x[k + 4]) for k in range(4)])
    b = [csub(x[k], x[k + 4]) for k in range(4)]
    b1 = ((b[1][0] + b[1][1]) * root, (b[1][1] - b[1][0]) * root)
    b3 = ((b[3][1] - b[3][0]) * root, (b[3][0] + b[3][1]) * -root)
    odd = dft4([b[0], b1, turn(b[2]), b3])
    return [(even, odd)[d % 2][d // 2] for d in range(8)]


def doppler_channel(c, x_ref, wide_ref, dft_ref, cos_ref, sin_ref, z_ref, acc_ref):
    for unit in range(2):
        for half in range(2):
            cols = slice(128 * half, 128 * half + 128)
            rows = slice(16 * unit, 16 * unit + 16)
            x = [tuple(x_ref(pb, q)[rows, cols].astype(F32) for q in range(2)) for pb in range(8)]
            for d, (re, im) in enumerate(dft8(x)):
                cos, sin = cos_ref[d : d + 1, cols], sin_ref[d : d + 1, cols]
                at = slice(128 * unit + 16 * d, 128 * unit + 16 * d + 16)
                z_ref[at, 128 * half : 128 * half + 128] = (re * cos + im * sin).astype(BF16)
                z_ref[at, 256 + 128 * half : 384 + 128 * half] = (im * cos - re * sin).astype(BF16)
    spec = lax.dot_general(
        dft_ref[...], z_ref[...], (((1,), (1,)), ((), ())), preferred_element_type=F32
    )
    for b in range(2):
        real, imag = (wide_ref[(q * 2 + b) * 8 + c] for q in range(2))
        for unit in range(2):
            cols = slice(128 * unit, 128 * unit + 128)
            re, im = spec[:256, cols], spec[256:, cols]
            acc_ref[0, b, 8:264, cols] += real * re - imag * im
            acc_ref[1, b, 8:264, cols] += real * im + imag * re


def widen(i, weight_ref, wide_ref):
    lane = lax.broadcasted_iota(jnp.int32, (16, 128), 1)
    keep = lane // 8 == lax.broadcasted_iota(jnp.int32, (16, 128), 0)
    spread = (
        lax.broadcasted_iota(jnp.int32, (128, 128), 0) % 8
        == lax.broadcasted_iota(jnp.int32, (128, 128), 1) // 16
    )
    spread = jnp.where(spread, 1.0, 0.0).astype(BF16)
    w = jnp.concatenate(
        [
            jnp.where(keep, weight_ref[source, half, pl.ds(i, 1), :], 0.0)
            for source in range(8)
            for half in range(2)
        ],
        axis=0,
    )
    high = w.astype(BF16)
    rest = w - high.astype(F32)
    mid = rest.astype(BF16)
    low = (rest - mid.astype(F32)).astype(BF16)
    wide_ref[i] = sum(jnp.dot(part, spread, preferred_element_type=F32) for part in (low, mid, high))


def pack_block(j, acc_ref, out_ref):
    for unit in range(2):
        for q in range(2):
            both = jnp.concatenate(
                [
                    acc_ref[q, b, 32 * j + 7 : 32 * j + 7 + ROWS, 128 * unit : 128 * unit + 128]
                    for b in range(2)
                ],
                axis=0,
            )
            out_ref[unit, :, 128 * q : 128 * q + 128] = both.astype(BF16)


def make_taps(replica_ref, taps_ref):
    period = (
        lax.broadcasted_iota(jnp.int32, (16, 128), 0)
        == lax.broadcasted_iota(jnp.int32, (16, 128), 1) % 16
    )
    period = jnp.where(period, 1.0, 0.0).astype(F32)
    tables = []
    for q in range(2):
        row = jnp.concatenate(
            [replica_ref[q : q + 1, :].astype(F32), jnp.zeros((1, 128), F32)], axis=1
        )
        shifted = pltpu.roll(jnp.broadcast_to(row, (16, 384)), 0, 1, stride=1, stride_axis=0)
        tables.append(
            lax.dot_general(
                shifted.astype(BF16),
                period.astype(BF16),
                (((0,), (0,)), ((), ())),
                preferred_element_type=F32,
            )
        )
    lane = lax.broadcasted_iota(jnp.int32, (16, 128), 1) // 16
    for j in range(17):
        real, imag = (t[16 * j : 16 * j + 16] for t in tables)
        for d in range(8):
            keep = lane == d
            re, im = jnp.where(keep, real, 0.0), jnp.where(keep, imag, 0.0)
            from_real = jnp.concatenate([re, -im], axis=1).astype(BF16)
            from_imag = jnp.concatenate([im, re], axis=1).astype(BF16)
            taps_ref[j, 16 * d : 16 * d + 16, :] = from_real
            taps_ref[j, 128 + 16 * d : 144 + 16 * d, :] = from_imag


def compress(y_ref, taps_ref, sum_ref):
    depth = 2 * ROWS
    third = UNITS // 3

    def gates(block, first, count):
        x = jnp.concatenate(
            [
                y_ref[pl.ds(third * block + first + k, third)].reshape(third * depth, 256)
                for k in range(count)
            ],
            axis=1,
        )
        w = taps_ref[pl.ds(first, count)].reshape(256 * count, 256)
        return jnp.dot(x, w, preferred_element_type=F32)

    for block in range(3):
        rows = slice(block * third * depth, (block + 1) * third * depth)
        sum_ref[rows] = gates(block, 0, 5)
        for first in (5, 9, 13):
            sum_ref[rows] += gates(block, first, 4)


def frame(first_block, sum_ref, frame_ref):
    for unit in range(UNITS):
        for q in range(2):
            for b in range(2):
                for half in range(2):
                    start = (unit * 2 + b) * ROWS + half
                    value = sum_ref[start : start + 33, 128 * q : 128 * q + 128]
                    if unit == 0:
                        value = jnp.where(first_block, 0.0, value)
                    at = pl.ds(unit * 8 + q * 4 + b * 2 + half, 33, stride=8 * UNITS)
                    frame_ref[at, :] = value


def cut(base, shift, frame_ref):
    lane = lax.broadcasted_iota(jnp.int32, (8, 128), 1)
    gate = lane & 15
    gate_shift = shift & 15
    near_row, near_gate = lane >= shift - gate_shift, gate >= gate_shift
    f = [frame_ref[base + step] for step in (0, 1, UNITS, UNITS + 1)]
    z = jnp.where(
        near_row, jnp.where(near_gate, f[0], f[1]), jnp.where(near_gate, f[2], f[3])
    )
    return jnp.where(
        gate < 16 - gate_shift,
        pltpu.roll(z, (128 - shift) & 127, 1),
        pltpu.roll(z, (144 - shift) & 127, 1),
    )


CHUNKS = 4
PER = 8 // CHUNKS


def beams_kernel(
    echo_hbm,
    weights_ref,
    replica_ref,
    dft_hbm,
    cos_ref,
    sin_ref,
    codes_ref,
    tiles_ref,
    echo_ref,
    dft_ref,
    weight_ref,
    frame_ref,
    out_tile,
    out_strip,
    in_strip,
    all_weights,
    wide_ref,
    z_ref,
    acc_ref,
    out_block,
    y_ref,
    taps_ref,
    sum_ref,
    strip_sent,
    strip_here,
    strip_own,
    weight_sent,
    weight_here,
    block_sent,
    block_here,
    halo_sent,
    halo_here,
    edge_sent,
    edge_here,
    echo_loaded,
    dft_loaded,
    tile_sent,
    tile_here,
    row_here,
):
    me, g = lax.axis_index("pulse"), lax.axis_index("gate")
    gates = lax.axis_size("gate")
    barrier = pltpu.get_barrier_semaphore()

    def at(pulse, gate):
        return dict(device_id=(pulse, gate), device_id_type=pl.DeviceIdType.MESH)

    def peer(k):
        return lax.rem(me + k, 8)

    def load(chunk):
        channels = pl.ds(chunk * PER, PER)
        return pltpu.make_async_copy(
            echo_hbm.at[:, channels], echo_ref.at[:, channels], echo_loaded.at[chunk]
        )

    def load_dft():
        return pltpu.make_async_copy(dft_hbm, dft_ref, dft_loaded)

    for chunk in range(CHUNKS):
        load(chunk).start()
    load_dft().start()
    for k in range(1, 8):
        pl.semaphore_signal(barrier, inc=1, **at(peer(k), g))
    for k in range(1, gates):
        pl.semaphore_signal(barrier, inc=1, **at(me, lax.rem(g + k, gates)))

    def strip(chunk, target, source):
        return pltpu.make_async_remote_copy(
            src_ref=out_strip.at[chunk, target],
            dst_ref=in_strip.at[chunk, source],
            send_sem=strip_sent.at[chunk, target],
            recv_sem=strip_here.at[chunk, source],
            **at(target, g),
        )

    def own_strip(chunk):
        return pltpu.make_async_copy(
            out_strip.at[chunk, me], in_strip.at[chunk, me], strip_own.at[chunk]
        )

    def weight(target, source):
        return pltpu.make_async_remote_copy(
            src_ref=weight_ref,
            dst_ref=all_weights.at[source],
            send_sem=weight_sent.at[target],
            recv_sem=weight_here.at[source],
            **at(target, g),
        )

    def block(target, source):
        return pltpu.make_async_remote_copy(
            src_ref=out_block.at[target],
            dst_ref=y_ref.at[pl.ds(1 + 2 * source, 2)],
            send_sem=block_sent.at[target],
            recv_sem=block_here.at[source],
            **at(target, g),
        )

    def halo(source):
        return pltpu.make_async_remote_copy(
            src_ref=y_ref.at[pl.ds(1 + 2 * source, 2)],
            dst_ref=y_ref.at[pl.ds(17 + 2 * source, 2)],
            send_sem=halo_sent.at[source],
            recv_sem=halo_here.at[source],
            **at(me, g - 1),
        )

    def edge(which):
        return pltpu.make_async_remote_copy(
            src_ref=y_ref.at[(1, 16)[which]],
            dst_ref=y_ref.at[(33, 0)[which]],
            send_sem=edge_sent.at[which],
            recv_sem=edge_here.at[which],
            **at(me, (g - 2, g + 1)[which]),
        )

    def turn_chunk(chunk):
        load(chunk).wait()
        for c in range(PER):
            for q in range(2):
                turned = echo_ref[q, chunk * PER + c].T
                out_strip[chunk, :, q, c] = turned.reshape(8, 32, 256)

    def send_chunk(chunk):
        for k in range(1, 8):
            strip(chunk, peer(k), me).start()
        own_strip(chunk).start()

    for half in range(2):
        weight_ref[half] = weights_ref[:, 128 * half : 128 * half + 128]
    turn_chunk(0)
    pl.semaphore_wait(barrier, 7 + gates - 1)
    send_chunk(0)
    for k in range(1, 8):
        pl.semaphore_signal(row_here, inc=1, **at(peer(k), g))
    for k in range(1, 8):
        weight(peer(k), me).start()

    def turn_and_send(chunk, carry):
        turn_chunk(chunk)
        send_chunk(chunk)
        return carry

    lax.fori_loop(1, CHUNKS, turn_and_send, 0)

    all_weights[me] = weight_ref[...]
    acc_ref[...] = jnp.zeros_like(acc_ref)
    nothing = jnp.zeros((2 * ROWS, 256), BF16)

    @pl.when(g == 0)
    def _():
        y_ref[0] = nothing

    @pl.when(g == gates - 1)
    def _():
        for unit in range(17, 33):
            y_ref[unit] = nothing

    @pl.when(g >= gates - 2)
    def _():
        y_ref[33] = nothing

    make_taps(replica_ref, taps_ref)
    for k in range(1, 8):
        weight(me, peer(k)).wait_recv()

    def widen_step(i, carry):
        widen(i, all_weights, wide_ref)
        return carry

    lax.fori_loop(0, 32, widen_step, 0)

    load_dft().wait()

    def doppler_chunk(chunk, carry):
        own_strip(chunk).wait()
        for k in range(1, 8):
            strip(chunk, me, peer(k)).wait_recv()

        def one(c, inner):
            doppler_channel(
                chunk * PER + c,
                lambda pb, q: in_strip.at[chunk, pb, q, c],
                wide_ref,
                dft_ref,
                cos_ref,
                sin_ref,
                z_ref,
                acc_ref,
            )
            return inner

        return lax.fori_loop(0, PER, one, carry)

    lax.fori_loop(0, CHUNKS, doppler_chunk, 0)

    for j in range(8):

        @pl.when(me == j)
        def _():
            pack_block(j, acc_ref, y_ref.at[pl.ds(1 + 2 * j, 2)])

        @pl.when(me != j)
        def _():
            pack_block(j, acc_ref, out_block.at[j])
            block(j, me).start()

    def pass_on(source):
        @pl.when(g > 0)
        def _():
            halo(source).start()

        @pl.when((source == 0) & (g > 1))
        def _():
            edge(0).start()

        @pl.when((source == 7) & (g < gates - 1))
        def _():
            edge(1).start()

    pass_on(me)

    def arrive(k, carry):
        source = lax.rem(me + k, 8)
        block(me, source).wait_recv()
        pass_on(source)
        return carry

    lax.fori_loop(1, 8, arrive, 0)

    @pl.when(g < gates - 1)
    def _():
        for source in range(8):
            halo(source).wait_recv()

    @pl.when(g < gates - 2)
    def _():
        edge(0).wait_recv()

    @pl.when(g > 0)
    def _():
        edge(1).wait_recv()

    compress(y_ref, taps_ref, sum_ref)
    frame(g == 0, sum_ref, frame_ref.reshape(33 * UNITS * 8, 128))

    pl.semaphore_wait(row_here, 7)
    devices = 8 * gates
    here = me * gates + g

    def cut_block(owner):
        tiles = []
        for slot in range(5):
            code = codes_ref[owner * 5 + slot]
            tile = cut(lax.shift_right_logical(code, 8), code & 127, frame_ref)
            tiles.append(jnp.where(code & 128 != 0, tile, 0.0))
        return jnp.concatenate(tiles, axis=0).astype(BF16)

    def tile(owner, holder):
        return pltpu.make_async_remote_copy(
            src_ref=out_tile.at[owner],
            dst_ref=tiles_ref.at[holder],
            send_sem=tile_sent,
            recv_sem=tile_here,
            **at(owner // gates, lax.rem(owner, gates)),
        )

    def cut_and_send(k, carry):
        owner = lax.rem(here + k * 45, devices)
        out_tile[owner] = cut_block(owner)
        tile(owner, here).start()
        return carry

    lax.fori_loop(1, devices, cut_and_send, 0)
    tiles_ref[here] = cut_block(here)

    @pl.when(g > 0)
    def _():
        for source in range(8):
            halo(source).wait_send()

    @pl.when(g > 1)
    def _():
        edge(0).wait_send()

    @pl.when(g < gates - 1)
    def _():
        edge(1).wait_send()

    for k in range(1, 8):
        weight(peer(k), me).wait_send()
        block(peer(k), me).wait_send()

    def sent(chunk, carry):
        for k in range(1, 8):
            strip(chunk, peer(k), me).wait_send()
        return carry

    lax.fori_loop(0, CHUNKS, sent, 0)
    everyone = pltpu.make_async_remote_copy(
        src_ref=out_tile.at[pl.ds(0, devices - 1)],
        dst_ref=tiles_ref.at[pl.ds(0, devices - 1)],
        send_sem=tile_sent,
        recv_sem=tile_here,
        **at(me, g),
    )
    everyone.wait_recv()
    everyone.wait_send()


def tiles(echoes, weights, replica, codes, owners):
    dft, cos, sin = tables()
    dma = pltpu.SemaphoreType.DMA
    hbm = pl.BlockSpec(memory_space=pltpu.HBM)
    return pl.pallas_call(
        beams_kernel,
        out_shape=jax.ShapeDtypeStruct((owners, ROWS, 128), BF16),
        in_specs=[hbm, VMEM, VMEM, hbm, VMEM, VMEM, SMEM],
        out_specs=VMEM,
        scratch_shapes=[
            pltpu.VMEM((2, 8, 256, 256), BF16),
            pltpu.VMEM((512, 512), BF16),
            pltpu.VMEM((2, 32, 128), F32),
            pltpu.VMEM((33 * UNITS, 8, 128), F32),
            pltpu.VMEM((owners, ROWS, 128), BF16),
            pltpu.VMEM((CHUNKS, 8, 2, PER, 32, 256), BF16),
            pltpu.VMEM((CHUNKS, 8, 2, PER, 32, 256), BF16),
            pltpu.VMEM((8, 2, 32, 128), F32),
            pltpu.VMEM((32, 256, 128), F32),
            pltpu.VMEM((256, 512), BF16),
            pltpu.VMEM((2, 2, 272, 256), F32),
            pltpu.VMEM((8, 2, 2 * ROWS, 256), BF16),
            pltpu.VMEM((34, 2 * ROWS, 256), BF16),
            pltpu.VMEM((17, 256, 256), BF16),
            pltpu.VMEM((UNITS * 2 * ROWS, 256), F32),
            dma((CHUNKS, 8)),
            dma((CHUNKS, 8)),
            dma((CHUNKS,)),
            dma((8,)),
            dma((8,)),
            dma((8,)),
            dma((8,)),
            dma((8,)),
            dma((8,)),
            dma((2,)),
            dma((2,)),
            dma((CHUNKS,)),
            dma(()),
            dma(()),
            dma(()),
            pltpu.SemaphoreType.REGULAR,
        ],
        compiler_params=params(48, collective_id=0, has_side_effects=True),
        cost_estimate=pl.CostEstimate(flops=6 * 10**9, bytes_accessed=8 << 20, transcendentals=0),
    )(echoes, weights, replica, jnp.asarray(dft), jnp.asarray(cos), jnp.asarray(sin), codes)


def rows_kernel(tiles_ref, out_ref, in_ref):
    slots = out_ref.shape[0]
    in_ref[...] = tiles_ref[...].reshape(8 * slots, 128).astype(F32)
    for k in range(8):
        out_ref[:, 128 * k : 128 * k + 128] = in_ref[pl.ds(k, slots, stride=8), :]


def params(mib, **more):
    return pltpu.CompilerParams(vmem_limit_bytes=mib << 20, **more)


def local(echoes, replica, beam_weights, track_doppler, track_gate, track_owner):
    pulse_devices, gate_devices = lax.axis_size("pulse"), lax.axis_size("gate")
    owners = pulse_devices * gate_devices
    tracks = track_owner.shape[0]
    capacity = 5
    row_in, gate_in = track_doppler % 256, track_gate % 256 + 8
    base = row_in // 8 * UNITS + gate_in // 16
    shift = row_in % 8 * 16 + gate_in % 16
    order = jnp.arange(tracks, dtype=jnp.int32)
    earlier = (track_owner[:, None] == track_owner[None, :]) & (order[None, :] < order[:, None])
    rank = jnp.sum(earlier.astype(jnp.int32), axis=1, dtype=jnp.int32)
    slot = track_owner * capacity + rank

    place = jnp.arange(owners * capacity, dtype=jnp.int32)
    code = base * 256 + shift + 128
    codes = jnp.sum(jnp.where(slot[None, :] == place[:, None], code[None, :], 0), axis=1, dtype=jnp.int32)
    received = tiles(echoes, beam_weights.reshape(32, 256), replica, codes, owners)
    return pl.pallas_call(
        rows_kernel,
        out_shape=jax.ShapeDtypeStruct((owners * capacity, 1024), F32),
        in_specs=[VMEM],
        out_specs=VMEM,
        scratch_shapes=[pltpu.VMEM((owners * capacity * 8, 128), F32)],
        compiler_params=params(16),
    )(received)


def solution(mesh):
    return jax.shard_map(
        local,
        mesh=mesh,
        in_specs=(
            P(None, None, "pulse", "gate"),
            P(),
            P(None, None, None, "pulse"),
            P(("pulse", "gate")),
            P(("pulse", "gate")),
            P(("pulse", "gate")),
        ),
        out_specs=P(("pulse", "gate"), None),
        check_vma=False,
    )
```

```python
import functools
import math

import jax
import jax.numpy as jnp
import numpy as np
from jax import lax
from jax.experimental import pallas as pl
from jax.experimental.pallas import tpu as pltpu
from jax.sharding import PartitionSpec as P

F32 = jnp.float32
BF16 = jnp.bfloat16
UNITS = 18
ROWS = 40
VMEM = pl.BlockSpec(memory_space=pltpu.VMEM)
SMEM = pl.BlockSpec(memory_space=pltpu.SMEM)


def tables():
    angle = 2.0 * np.pi * ((np.arange(256)[:, None] * np.arange(256)[None, :]) % 256) / 256.0
    cos, sin = np.cos(angle), np.sin(angle)
    dft = np.block([[cos, sin], [-sin, cos]]).astype(jnp.bfloat16)
    twist = 2.0 * np.pi * (np.arange(8)[:, None] * np.arange(256)[None, :]) / 2048.0
    scale = 1.0 / 1024.0
    return dft, np.stack([np.cos(twist) * scale, np.sin(twist) * scale]).astype(np.float32)


def cadd(a, b):
    return (a[0] + b[0], a[1] + b[1])


def csub(a, b):
    return (a[0] - b[0], a[1] - b[1])


def turn(a):
    return (a[1], -a[0])


def dft4(a):
    e0, e1 = cadd(a[0], a[2]), csub(a[0], a[2])
    f0, f1 = cadd(a[1], a[3]), turn(csub(a[1], a[3]))
    return [cadd(e0, f0), cadd(e1, f1), csub(e0, f0), csub(e1, f1)]


def dft8(x):
    root = math.sqrt(0.5)
    even = dft4([cadd(x[k], x[k + 4]) for k in range(4)])
    b = [csub(x[k], x[k + 4]) for k in range(4)]
    b1 = ((b[1][0] + b[1][1]) * root, (b[1][1] - b[1][0]) * root)
    b3 = ((b[3][1] - b[3][0]) * root, (b[3][0] + b[3][1]) * -root)
    odd = dft4([b[0], b1, turn(b[2]), b3])
    return [(even, odd)[d % 2][d // 2] for d in range(8)]


def doppler_pair(pair, x_ref, wide_ref, dft_ref, twist_ref, z_ref, acc_ref):
    for c in range(2):
        for half in range(2):
            cols = slice(128 * half, 128 * half + 128)
            x = [tuple(x_ref[pb, q, c, :, cols].astype(F32) for q in range(2)) for pb in range(8)]
            for d, (re, im) in enumerate(dft8(x)):
                cos, sin = (twist_ref[k, d : d + 1, cols] for k in range(2))
                at = slice(128 * c + 16 * d, 128 * c + 16 * d + 16)
                z_ref[at, 128 * half : 128 * half + 128] = (re * cos + im * sin).astype(BF16)
                z_ref[at, 256 + 128 * half : 384 + 128 * half] = (im * cos - re * sin).astype(BF16)
    spec = lax.dot_general(
        dft_ref[...], z_ref[...], (((1,), (1,)), ((), ())), preferred_element_type=F32
    )
    for b in range(2):
        real, imag = 0.0, 0.0
        for c in range(2):
            w_re, w_im = (wide_ref[(q * 2 + b) * 8 + 2 * pair + c] for q in range(2))
            cols = slice(128 * c, 128 * c + 128)
            re, im = spec[:256, cols], spec[256:, cols]
            real += w_re * re - w_im * im
            imag += w_re * im + w_im * re
        acc_ref[0, b, 8:264] += real
        acc_ref[1, b, 8:264] += imag


def widen(i, weight_ref, wide_ref):
    lane = lax.broadcasted_iota(jnp.int32, (16, 128), 1)
    keep = lane // 8 == lax.broadcasted_iota(jnp.int32, (16, 128), 0)
    spread = (
        lax.broadcasted_iota(jnp.int32, (128, 128), 0) % 8
        == lax.broadcasted_iota(jnp.int32, (128, 128), 1) // 16
    )
    spread = jnp.where(spread, 1.0, 0.0).astype(BF16)
    w = jnp.concatenate(
        [
            jnp.where(keep, weight_ref[source, half, pl.ds(i, 1), :], 0.0)
            for source in range(8)
            for half in range(2)
        ],
        axis=0,
    )
    high = w.astype(BF16)
    rest = w - high.astype(F32)
    mid = rest.astype(BF16)
    low = (rest - mid.astype(F32)).astype(BF16)
    wide_ref[i] = sum(jnp.dot(part, spread, preferred_element_type=F32) for part in (low, mid, high))


def pack_block(j, acc_ref, out_ref):
    for q in range(2):
        both = jnp.concatenate(
            [acc_ref[q, b, 32 * j + 7 : 32 * j + 7 + ROWS] for b in range(2)], axis=0
        )
        out_ref[:, 128 * q : 128 * q + 128] = both.astype(BF16)


def make_taps(replica_ref, taps_ref):
    period = (
        lax.broadcasted_iota(jnp.int32, (16, 128), 0)
        == lax.broadcasted_iota(jnp.int32, (16, 128), 1) % 16
    )
    period = jnp.where(period, 1.0, 0.0).astype(F32)
    tables = []
    for q in range(2):
        row = jnp.concatenate(
            [replica_ref[q : q + 1, :].astype(F32), jnp.zeros((1, 128), F32)], axis=1
        )
        shifted = pltpu.roll(jnp.broadcast_to(row, (16, 384)), 0, 1, stride=1, stride_axis=0)
        tables.append(
            lax.dot_general(
                shifted.astype(BF16),
                period.astype(BF16),
                (((0,), (0,)), ((), ())),
                preferred_element_type=F32,
            )
        )
    lane = lax.broadcasted_iota(jnp.int32, (16, 128), 1) // 16
    for j in range(17):
        real, imag = (t[16 * j : 16 * j + 16] for t in tables)
        for d in range(8):
            keep = lane == d
            re, im = jnp.where(keep, real, 0.0), jnp.where(keep, imag, 0.0)
            from_real = jnp.concatenate([re, -im], axis=1).astype(BF16)
            from_imag = jnp.concatenate([im, re], axis=1).astype(BF16)
            taps_ref[j, 16 * d : 16 * d + 16, :] = from_real
            taps_ref[j, 128 + 16 * d : 144 + 16 * d, :] = from_imag


def compress(parity, y_ref, taps_ref, sum_ref):
    half, depth = UNITS // 2, 2 * ROWS
    for out in range(2):
        odd = (parity - out) % 2
        skip = out * (1 - parity)
        total = 9 - odd

        def part(first, count):
            x = jnp.concatenate(
                [
                    y_ref[parity, pl.ds(skip + first + k, half)].reshape(half * depth, 256)
                    for k in range(count)
                ],
                axis=1,
            )
            w = jnp.concatenate([taps_ref[odd + 2 * (first + k)] for k in range(count)], axis=0)
            return jnp.dot(x, w, preferred_element_type=F32)

        for first in range(0, 8, 4):
            count = 5 if first == 4 and total == 9 else 4
            if parity == 1 and first == 0:
                sum_ref[out] = part(first, count)
            else:
                sum_ref[out] += part(first, count)


def frame(first_block, sum_ref, frame_ref):
    for unit in range(UNITS):
        for q in range(2):
            for b in range(2):
                for half in range(2):
                    start = (unit // 2 * 2 + b) * ROWS + half
                    value = sum_ref[unit % 2, start : start + 33, 128 * q : 128 * q + 128]
                    if unit == 0:
                        value = jnp.where(first_block, 0.0, value)
                    at = pl.ds(unit * 8 + q * 4 + b * 2 + half, 33, stride=8 * UNITS)
                    frame_ref[at, :] = value


def slot_codes(doppler, gate, owner, slots):
    row, col = doppler & 255, (gate & 255) + 8
    base = lax.shift_right_logical(row, 3) * UNITS + lax.shift_right_logical(col, 4)
    code = (base * 256 + 128 + (row & 7) * 16 + (col & 15)).astype(F32)
    owner = owner.astype(F32)
    tracks = owner.shape[1]
    column = jnp.broadcast_to(owner, (8, tracks)).T[:, :1]
    square = (tracks, tracks)
    before = lax.broadcasted_iota(jnp.int32, square, 0) < lax.broadcasted_iota(jnp.int32, square, 1)
    same = jnp.where((column == owner) & before, 1.0, 0.0)
    slot = owner * 5.0 + jnp.sum(same, axis=0, keepdims=True)
    both = jnp.concatenate([slot, code, jnp.zeros((6, tracks), F32)], axis=0).T
    place = lax.broadcasted_iota(jnp.int32, (tracks, slots), 1).astype(F32)
    found = jnp.where(both[:, :1] == place, both[:, 1:2], 0.0)
    return jnp.sum(found, axis=0, keepdims=True).astype(jnp.int32)


def cut(base, shift, frame_ref):
    lane = lax.broadcasted_iota(jnp.int32, (8, 128), 1)
    gate = lane & 15
    gate_shift = shift & 15
    near_row, near_gate = lane >= shift - gate_shift, gate >= gate_shift
    f = [frame_ref[base + step] for step in (0, 1, UNITS, UNITS + 1)]
    z = jnp.where(
        near_row, jnp.where(near_gate, f[0], f[1]), jnp.where(near_gate, f[2], f[3])
    )
    return jnp.where(
        gate < 16 - gate_shift,
        pltpu.roll(z, (128 - shift) & 127, 1),
        pltpu.roll(z, (144 - shift) & 127, 1),
    )


PAIRS = 4


def tiles_kernel(
    echo_hbm,
    weights_hbm,
    replica_hbm,
    dft_hbm,
    twist_hbm,
    doppler_hbm,
    gate_hbm,
    owner_hbm,
    tiles_ref,
    echo_ref,
    weights_ref,
    replica_ref,
    dft_ref,
    twist_ref,
    track_ref,
    code_ref,
    codes_ref,
    weight_ref,
    frame_ref,
    out_tile,
    out_strip,
    in_strip,
    all_weights,
    wide_ref,
    z_ref,
    acc_ref,
    out_block,
    y_ref,
    taps_ref,
    sum_ref,
    strip_sent,
    strip_here,
    strip_own,
    weight_sent,
    weight_here,
    block_sent,
    block_here,
    halo_sent,
    halo_here,
    edge_sent,
    edge_here,
    echo_loaded,
    loaded,
    code_moved,
    tile_sent,
    tile_here,
    row_here,
):
    me, g = lax.axis_index("pulse"), lax.axis_index("gate")
    gates = lax.axis_size("gate")
    barrier = pltpu.get_barrier_semaphore()

    def at(pulse, gate):
        return dict(device_id=(pulse, gate), device_id_type=pl.DeviceIdType.MESH)

    def peer(k):
        return lax.rem(me + k, 8)

    def load(pair):
        channels = pl.ds(pair * 2, 2)
        return pltpu.make_async_copy(
            echo_hbm.at[:, channels], echo_ref.at[:, channels], echo_loaded.at[pair]
        )

    small = [
        (weights_hbm, weights_ref),
        (replica_hbm, replica_ref),
        (dft_hbm, dft_ref),
        (twist_hbm, twist_ref),
        (doppler_hbm, track_ref.at[0]),
        (gate_hbm, track_ref.at[1]),
        (owner_hbm, track_ref.at[2]),
    ]
    loads = [
        pltpu.make_async_copy(source, target, loaded.at[k])
        for k, (source, target) in enumerate(small)
    ]
    for k in range(1, 8):
        pl.semaphore_signal(barrier, inc=1, **at(peer(k), g))
    for k in range(1, gates):
        pl.semaphore_signal(barrier, inc=1, **at(me, lax.rem(g + k, gates)))
    for pair in range(PAIRS):
        load(pair).start()
    for copy in loads:
        copy.start()

    def strip(unit, pair, target, source):
        return pltpu.make_async_remote_copy(
            src_ref=out_strip.at[unit, pair, target],
            dst_ref=in_strip.at[unit, pair, source],
            send_sem=strip_sent.at[unit, pair, target],
            recv_sem=strip_here.at[unit, pair, source],
            **at(target, g),
        )

    def own_strip(unit, pair):
        return pltpu.make_async_copy(
            out_strip.at[unit, pair, me], in_strip.at[unit, pair, me], strip_own.at[unit, pair]
        )

    def weight(target, source):
        return pltpu.make_async_remote_copy(
            src_ref=weight_ref,
            dst_ref=all_weights.at[source],
            send_sem=weight_sent.at[target],
            recv_sem=weight_here.at[source],
            **at(target, g),
        )

    def block(u, target, source):
        return pltpu.make_async_remote_copy(
            src_ref=out_block.at[u, target],
            dst_ref=y_ref.at[1 - u, source + u],
            send_sem=block_sent.at[u, target],
            recv_sem=block_here.at[u, source],
            **at(target, g),
        )

    def halo(u, source):
        return pltpu.make_async_remote_copy(
            src_ref=y_ref.at[1 - u, source + u],
            dst_ref=y_ref.at[1 - u, source + u + 8],
            send_sem=halo_sent.at[u, source],
            recv_sem=halo_here.at[u, source],
            **at(me, g - 1),
        )

    def edge(u):
        return pltpu.make_async_remote_copy(
            src_ref=y_ref.at[1 - u, (0, 8)[u]],
            dst_ref=y_ref.at[1 - u, (16, 0)[u]],
            send_sem=edge_sent.at[u],
            recv_sem=edge_here.at[u],
            **at(me, (g - 2, g + 1)[u]),
        )

    def turn(pair):
        load(pair).wait()
        for c in range(2):
            for q in range(2):
                turned = echo_ref[q, pair * 2 + c].T.reshape(8, 2, 16, 256)
                for unit in range(2):
                    out_strip[unit, pair, :, q, c] = turned[:, unit]

    def send(unit, pair):
        for k in range(1, 8):
            strip(unit, pair, peer(k), me).start()
        own_strip(unit, pair).start()

    loads[0].wait()
    for half in range(2):
        weight_ref[half] = weights_ref[:, 128 * half : 128 * half + 128]
    turn(0)
    pl.semaphore_wait(barrier, 7 + gates - 1)
    for k in range(1, 8):
        weight(peer(k), me).start()
    send(0, 0)
    for k in range(1, 8):
        pl.semaphore_signal(row_here, inc=1, **at(peer(k), g))

    def turn_and_send(pair, carry):
        turn(pair)
        send(0, pair)
        return carry

    def send_second(pair, carry):
        send(1, pair)
        return carry

    lax.fori_loop(1, PAIRS, turn_and_send, 0)
    lax.fori_loop(0, PAIRS, send_second, 0)

    for copy in loads[1:]:
        copy.wait()
    code_ref[...] = slot_codes(track_ref[0], track_ref[1], track_ref[2], code_ref.shape[1])
    move = pltpu.make_async_copy(code_ref, codes_ref, code_moved)
    move.start()
    all_weights[me] = weight_ref[...]
    nothing = jnp.zeros((2 * ROWS, 256), BF16)

    @pl.when(g == 0)
    def _():
        y_ref[0, 0] = nothing

    @pl.when(g == gates - 1)
    def _():
        for k in range(8):
            y_ref[1, 8 + k] = nothing
            y_ref[0, 9 + k] = nothing

    @pl.when(g >= gates - 2)
    def _():
        y_ref[1, 16] = nothing

    make_taps(replica_ref, taps_ref)
    for k in range(1, 8):
        weight(me, peer(k)).wait_recv()

    def widen_step(i, carry):
        widen(i, all_weights, wide_ref)
        return carry

    lax.fori_loop(0, 32, widen_step, 0)
    move.wait()

    for u in range(2):
        acc_ref[...] = jnp.zeros_like(acc_ref)

        def transform(pair, carry):
            own_strip(u, pair).wait()
            for k in range(1, 8):
                strip(u, pair, me, peer(k)).wait_recv()
            doppler_pair(
                pair, in_strip.at[u, pair], wide_ref, dft_ref, twist_ref, z_ref, acc_ref
            )
            return carry

        lax.fori_loop(0, PAIRS, transform, 0)

        for j in range(8):

            @pl.when(me == j)
            def _():
                pack_block(j, acc_ref, y_ref.at[1 - u, j + u])

            @pl.when(me != j)
            def _():
                pack_block(j, acc_ref, out_block.at[u, j])
                block(u, j, me).start()

    def pass_on(u, source):
        @pl.when(g > 0)
        def _():
            halo(u, source).start()

        if u == 0:

            @pl.when((source == 0) & (g > 1))
            def _():
                edge(0).start()

        else:

            @pl.when((source == 7) & (g < gates - 1))
            def _():
                edge(1).start()

    for u in range(2):
        pass_on(u, me)

        def arrive(k, carry):
            source = peer(k)
            block(u, me, source).wait_recv()
            pass_on(u, source)
            return carry

        lax.fori_loop(1, 8, arrive, 0)

    for u in range(2):

        @pl.when(g < gates - 1)
        def _():
            for source in range(8):
                halo(u, source).wait_recv()

        @pl.when((g < gates - 2, g > 0)[u])
        def _():
            edge(u).wait_recv()

        compress(1 - u, y_ref, taps_ref, sum_ref)

    frame(g == 0, sum_ref, frame_ref.reshape(33 * UNITS * 8, 128))

    pl.semaphore_wait(row_here, 7)
    devices = 8 * gates
    here = me * gates + g

    def cut_block(owner):
        tiles = []
        for slot in range(5):
            code = codes_ref[0, owner * 5 + slot]
            base = jnp.clip(lax.shift_right_logical(code, 8), 0, 32 * UNITS - 2)
            tile = cut(base, code & 127, frame_ref)
            tiles.append(jnp.where(code & 128 != 0, tile, 0.0))
        return jnp.concatenate(tiles, axis=0).astype(BF16)

    def tile(owner, holder):
        return pltpu.make_async_remote_copy(
            src_ref=out_tile.at[owner],
            dst_ref=tiles_ref.at[holder],
            send_sem=tile_sent,
            recv_sem=tile_here,
            **at(owner // gates, lax.rem(owner, gates)),
        )

    def cut_and_send(k, carry):
        owner = lax.rem(here + k * 45, devices)
        out_tile[owner] = cut_block(owner)
        tile(owner, here).start()
        return carry

    lax.fori_loop(1, devices, cut_and_send, 0)
    tiles_ref[here] = cut_block(here)

    for u in range(2):

        @pl.when(g > 0)
        def _():
            for source in range(8):
                halo(u, source).wait_send()

        @pl.when((g > 1, g < gates - 1)[u])
        def _():
            edge(u).wait_send()

    for k in range(1, 8):
        weight(peer(k), me).wait_send()
        for u in range(2):
            block(u, peer(k), me).wait_send()

    def sent(pair, carry):
        for k in range(1, 8):
            for u in range(2):
                strip(u, pair, peer(k), me).wait_send()
        return carry

    lax.fori_loop(0, PAIRS, sent, 0)
    everyone = pltpu.make_async_remote_copy(
        src_ref=out_tile.at[pl.ds(0, devices - 1)],
        dst_ref=tiles_ref.at[pl.ds(0, devices - 1)],
        send_sem=tile_sent,
        recv_sem=tile_here,
        **at(me, g),
    )
    everyone.wait_recv()
    everyone.wait_send()


def tiles(echoes, weights, replica, doppler, gate, owner, owners):
    dft, twist = tables()
    dma = pltpu.SemaphoreType.DMA
    hbm = pl.BlockSpec(memory_space=pltpu.HBM)
    return pl.pallas_call(
        tiles_kernel,
        out_shape=jax.ShapeDtypeStruct((owners, ROWS, 128), BF16),
        in_specs=[hbm] * 8,
        out_specs=VMEM,
        scratch_shapes=[
            pltpu.VMEM((2, 8, 256, 256), BF16),
            pltpu.VMEM((32, 256), F32),
            pltpu.VMEM((2, 256), BF16),
            pltpu.VMEM((512, 512), BF16),
            pltpu.VMEM((2, 8, 256), F32),
            pltpu.VMEM((3, 1, 256), jnp.int32),
            pltpu.VMEM((1, owners * 5), jnp.int32),
            pltpu.SMEM((1, owners * 5), jnp.int32),
            pltpu.VMEM((2, 32, 128), F32),
            pltpu.VMEM((33 * UNITS, 8, 128), F32),
            pltpu.VMEM((owners, ROWS, 128), BF16),
            pltpu.VMEM((2, PAIRS, 8, 2, 2, 16, 256), BF16),
            pltpu.VMEM((2, PAIRS, 8, 2, 2, 16, 256), BF16),
            pltpu.VMEM((8, 2, 32, 128), F32),
            pltpu.VMEM((32, 256, 128), F32),
            pltpu.VMEM((256, 512), BF16),
            pltpu.VMEM((2, 2, 272, 128), F32),
            pltpu.VMEM((2, 8, 2 * ROWS, 256), BF16),
            pltpu.VMEM((2, 17, 2 * ROWS, 256), BF16),
            pltpu.VMEM((17, 256, 256), BF16),
            pltpu.VMEM((2, UNITS * ROWS, 256), F32),
            dma((2, PAIRS, 8)),
            dma((2, PAIRS, 8)),
            dma((2, PAIRS)),
            dma((8,)),
            dma((8,)),
            dma((2, 8)),
            dma((2, 8)),
            dma((2, 8)),
            dma((2, 8)),
            dma((2,)),
            dma((2,)),
            dma((PAIRS,)),
            dma((7,)),
            dma(()),
            dma(()),
            dma(()),
            pltpu.SemaphoreType.REGULAR,
        ],
        compiler_params=params(60, collective_id=0, has_side_effects=True),
        cost_estimate=pl.CostEstimate(flops=6 * 10**9, bytes_accessed=8 << 20, transcendentals=0),
    )(echoes, weights, replica, jnp.asarray(dft), jnp.asarray(twist), doppler, gate, owner)


def rows_kernel(tiles_ref, out_ref, in_ref):
    slots = out_ref.shape[0]
    in_ref[...] = tiles_ref[...].reshape(8 * slots, 128).astype(F32)
    for k in range(8):
        out_ref[:, 128 * k : 128 * k + 128] = in_ref[pl.ds(k, slots, stride=8), :]


def params(mib, **more):
    return pltpu.CompilerParams(vmem_limit_bytes=mib << 20, **more)


def local(echoes, replica, beam_weights, track_doppler, track_gate, track_owner):
    pulse_devices, gate_devices = lax.axis_size("pulse"), lax.axis_size("gate")
    owners = pulse_devices * gate_devices
    tracks = track_owner.shape[0]
    capacity = 5
    rows = (x.reshape(1, tracks) for x in (track_doppler, track_gate, track_owner))
    received = tiles(echoes, beam_weights.reshape(32, 256), replica, *rows, owners)
    return pl.pallas_call(
        rows_kernel,
        out_shape=jax.ShapeDtypeStruct((owners * capacity, 1024), F32),
        in_specs=[VMEM],
        out_specs=VMEM,
        scratch_shapes=[pltpu.VMEM((owners * capacity * 8, 128), F32)],
        compiler_params=params(16),
    )(received)


def solution(mesh):
    return jax.shard_map(
        local,
        mesh=mesh,
        in_specs=(
            P(None, None, "pulse", "gate"),
            P(),
            P(None, None, None, "pulse"),
            P(("pulse", "gate")),
            P(("pulse", "gate")),
            P(("pulse", "gate")),
        ),
        out_specs=P(("pulse", "gate"), None),
        check_vma=False,
    )
```

```python
import functools
import math

import jax
import jax.numpy as jnp
import numpy as np
from jax import lax
from jax.experimental import pallas as pl
from jax.experimental.pallas import tpu as pltpu
from jax.sharding import PartitionSpec as P

F32 = jnp.float32
BF16 = jnp.bfloat16
UNITS = 18
ROWS = 40
VMEM = pl.BlockSpec(memory_space=pltpu.VMEM)
SMEM = pl.BlockSpec(memory_space=pltpu.SMEM)


def tables():
    angle = 2.0 * np.pi * ((np.arange(256)[:, None] * np.arange(256)[None, :]) % 256) / 256.0
    cos, sin = np.cos(angle), np.sin(angle)
    dft = np.block([[cos, sin], [-sin, cos]]).astype(jnp.bfloat16)
    twist = 2.0 * np.pi * (np.arange(8)[:, None] * np.arange(256)[None, :]) / 2048.0
    scale = 1.0 / 1024.0
    return dft, np.stack([np.cos(twist) * scale, np.sin(twist) * scale]).astype(np.float32)


def cadd(a, b):
    return (a[0] + b[0], a[1] + b[1])


def csub(a, b):
    return (a[0] - b[0], a[1] - b[1])


def turn(a):
    return (a[1], -a[0])


def dft4(a):
    e0, e1 = cadd(a[0], a[2]), csub(a[0], a[2])
    f0, f1 = cadd(a[1], a[3]), turn(csub(a[1], a[3]))
    return [cadd(e0, f0), cadd(e1, f1), csub(e0, f0), csub(e1, f1)]


def dft8(x):
    root = math.sqrt(0.5)
    even = dft4([cadd(x[k], x[k + 4]) for k in range(4)])
    b = [csub(x[k], x[k + 4]) for k in range(4)]
    b1 = ((b[1][0] + b[1][1]) * root, (b[1][1] - b[1][0]) * root)
    b3 = ((b[3][1] - b[3][0]) * root, (b[3][0] + b[3][1]) * -root)
    odd = dft4([b[0], b1, turn(b[2]), b3])
    return [(even, odd)[d % 2][d // 2] for d in range(8)]


def doppler_pair(pair, x_ref, wide_ref, dft_ref, twist_ref, z_ref, acc_ref):
    for c in range(2):
        for half in range(2):
            cols = slice(128 * half, 128 * half + 128)
            x = [tuple(x_ref[pb, q, c, :, cols].astype(F32) for q in range(2)) for pb in range(8)]
            for d, (re, im) in enumerate(dft8(x)):
                cos, sin = (twist_ref[k, d : d + 1, cols] for k in range(2))
                at = slice(128 * c + 16 * d, 128 * c + 16 * d + 16)
                z_ref[at, 128 * half : 128 * half + 128] = (re * cos + im * sin).astype(BF16)
                z_ref[at, 256 + 128 * half : 384 + 128 * half] = (im * cos - re * sin).astype(BF16)
    spec = lax.dot_general(
        dft_ref[...], z_ref[...], (((1,), (1,)), ((), ())), preferred_element_type=F32
    )
    for b in range(2):
        real, imag = 0.0, 0.0
        for c in range(2):
            w_re, w_im = (wide_ref[(q * 2 + b) * 8 + 2 * pair + c] for q in range(2))
            cols = slice(128 * c, 128 * c + 128)
            re, im = spec[:256, cols], spec[256:, cols]
            real += w_re * re - w_im * im
            imag += w_re * im + w_im * re
        acc_ref[0, b, 8:264] += real
        acc_ref[1, b, 8:264] += imag


def widen(i, weight_ref, wide_ref):
    lane = lax.broadcasted_iota(jnp.int32, (16, 128), 1)
    keep = lane // 8 == lax.broadcasted_iota(jnp.int32, (16, 128), 0)
    spread = (
        lax.broadcasted_iota(jnp.int32, (128, 128), 0) % 8
        == lax.broadcasted_iota(jnp.int32, (128, 128), 1) // 16
    )
    spread = jnp.where(spread, 1.0, 0.0).astype(BF16)
    w = jnp.concatenate(
        [
            jnp.where(keep, weight_ref[source, half, pl.ds(i, 1), :], 0.0)
            for source in range(8)
            for half in range(2)
        ],
        axis=0,
    )
    high = w.astype(BF16)
    rest = w - high.astype(F32)
    mid = rest.astype(BF16)
    low = (rest - mid.astype(F32)).astype(BF16)
    wide_ref[i] = sum(jnp.dot(part, spread, preferred_element_type=F32) for part in (low, mid, high))


def pack_block(j, acc_ref, out_ref):
    for q in range(2):
        both = jnp.concatenate(
            [acc_ref[q, b, 32 * j + 7 : 32 * j + 7 + ROWS] for b in range(2)], axis=0
        )
        out_ref[:, 128 * q : 128 * q + 128] = both.astype(BF16)


def make_taps(replica_ref, taps_ref):
    period = (
        lax.broadcasted_iota(jnp.int32, (16, 128), 0)
        == lax.broadcasted_iota(jnp.int32, (16, 128), 1) % 16
    )
    period = jnp.where(period, 1.0, 0.0).astype(F32)
    tables = []
    for q in range(2):
        row = jnp.concatenate(
            [replica_ref[q : q + 1, :].astype(F32), jnp.zeros((1, 128), F32)], axis=1
        )
        shifted = pltpu.roll(jnp.broadcast_to(row, (16, 384)), 0, 1, stride=1, stride_axis=0)
        tables.append(
            lax.dot_general(
                shifted.astype(BF16),
                period.astype(BF16),
                (((0,), (0,)), ((), ())),
                preferred_element_type=F32,
            )
        )
    lane = lax.broadcasted_iota(jnp.int32, (16, 128), 1) // 16
    for j in range(17):
        real, imag = (t[16 * j : 16 * j + 16] for t in tables)
        for d in range(8):
            keep = lane == d
            re, im = jnp.where(keep, real, 0.0), jnp.where(keep, imag, 0.0)
            from_real = jnp.concatenate([re, -im], axis=1).astype(BF16)
            from_imag = jnp.concatenate([im, re], axis=1).astype(BF16)
            taps_ref[j, 16 * d : 16 * d + 16, :] = from_real
            taps_ref[j, 128 + 16 * d : 144 + 16 * d, :] = from_imag


def compress(parity, y_ref, taps_ref, sum_ref):
    half, depth = UNITS // 2, 2 * ROWS
    for out in range(2):
        odd = (parity - out) % 2
        skip = out * (1 - parity)
        total = 9 - odd

        def part(first, count):
            x = jnp.concatenate(
                [
                    y_ref[parity, pl.ds(skip + first + k, half)].reshape(half * depth, 256)
                    for k in range(count)
                ],
                axis=1,
            )
            w = jnp.concatenate([taps_ref[odd + 2 * (first + k)] for k in range(count)], axis=0)
            return jnp.dot(x, w, preferred_element_type=F32)

        for first in range(0, 8, 4):
            count = 5 if first == 4 and total == 9 else 4
            if parity == 1 and first == 0:
                sum_ref[out] = part(first, count)
            else:
                sum_ref[out] += part(first, count)


def frame(first_block, sum_ref, frame_ref):
    for unit in range(UNITS):
        for q in range(2):
            for b in range(2):
                for half in range(2):
                    start = (unit // 2 * 2 + b) * ROWS + half
                    value = sum_ref[unit % 2, start : start + 33, 128 * q : 128 * q + 128]
                    if unit == 0:
                        value = jnp.where(first_block, 0.0, value)
                    at = pl.ds(unit * 8 + q * 4 + b * 2 + half, 33, stride=8 * UNITS)
                    frame_ref[at, :] = value


def slot_codes(doppler, gate, owner, slots):
    row, col = doppler & 255, (gate & 255) + 8
    base = lax.shift_right_logical(row, 3) * UNITS + lax.shift_right_logical(col, 4)
    code = (base * 256 + 128 + (row & 7) * 16 + (col & 15)).astype(F32)
    owner = owner.astype(F32)
    tracks = owner.shape[1]
    column = jnp.broadcast_to(owner, (8, tracks)).T[:, :1]
    square = (tracks, tracks)
    before = lax.broadcasted_iota(jnp.int32, square, 0) < lax.broadcasted_iota(jnp.int32, square, 1)
    same = jnp.where((column == owner) & before, 1.0, 0.0)
    slot = owner * 5.0 + jnp.sum(same, axis=0, keepdims=True)
    both = jnp.concatenate([slot, code, jnp.zeros((6, tracks), F32)], axis=0).T
    place = lax.broadcasted_iota(jnp.int32, (tracks, slots), 1).astype(F32)
    found = jnp.where(both[:, :1] == place, both[:, 1:2], 0.0)
    return jnp.sum(found, axis=0, keepdims=True).astype(jnp.int32)


def cut(base, shift, frame_ref):
    lane = lax.broadcasted_iota(jnp.int32, (8, 128), 1)
    gate = lane & 15
    gate_shift = shift & 15
    near_row, near_gate = lane >= shift - gate_shift, gate >= gate_shift
    f = [frame_ref[base + step] for step in (0, 1, UNITS, UNITS + 1)]
    z = jnp.where(
        near_row, jnp.where(near_gate, f[0], f[1]), jnp.where(near_gate, f[2], f[3])
    )
    return jnp.where(
        gate < 16 - gate_shift,
        pltpu.roll(z, (128 - shift) & 127, 1),
        pltpu.roll(z, (144 - shift) & 127, 1),
    )


PAIRS = 4
EARLY = 4
STEP = 3


def tiles_kernel(
    echo_hbm,
    weights_hbm,
    replica_hbm,
    dft_hbm,
    twist_hbm,
    doppler_hbm,
    gate_hbm,
    owner_hbm,
    tiles_ref,
    echo_ref,
    weights_ref,
    replica_ref,
    dft_ref,
    twist_ref,
    track_ref,
    code_ref,
    codes_ref,
    weight_ref,
    frame_ref,
    out_tile,
    out_strip,
    in_strip,
    all_weights,
    wide_ref,
    z_ref,
    acc_ref,
    out_block,
    y_ref,
    taps_ref,
    sum_ref,
    strip_sent,
    strip_here,
    strip_own,
    weight_sent,
    weight_here,
    block_sent,
    block_here,
    halo_sent,
    halo_here,
    edge_sent,
    edge_here,
    echo_loaded,
    loaded,
    code_moved,
    tile_sent,
    tile_here,
    row_here,
):
    me, g = lax.axis_index("pulse"), lax.axis_index("gate")
    gates = lax.axis_size("gate")
    barrier = pltpu.get_barrier_semaphore()

    def at(pulse, gate):
        return dict(device_id=(pulse, gate), device_id_type=pl.DeviceIdType.MESH)

    def peer(k):
        return lax.rem(me + k, 8)

    def load(pair):
        channels = pl.ds(pair * 2, 2)
        return pltpu.make_async_copy(
            echo_hbm.at[:, channels], echo_ref.at[:, channels], echo_loaded.at[pair]
        )

    small = [
        (weights_hbm, weights_ref),
        (replica_hbm, replica_ref),
        (dft_hbm, dft_ref),
        (twist_hbm, twist_ref),
        (doppler_hbm, track_ref.at[0]),
        (gate_hbm, track_ref.at[1]),
        (owner_hbm, track_ref.at[2]),
    ]
    loads = [
        pltpu.make_async_copy(source, target, loaded.at[k])
        for k, (source, target) in enumerate(small)
    ]
    for k in range(1, 8):
        pl.semaphore_signal(barrier, inc=1, **at(peer(k), g))
    for k in range(1, gates):
        pl.semaphore_signal(barrier, inc=1, **at(me, lax.rem(g + k, gates)))
    for pair in range(PAIRS):
        load(pair).start()
    for copy in loads:
        copy.start()

    def strip(unit, pair, target, source):
        return pltpu.make_async_remote_copy(
            src_ref=out_strip.at[unit, pair, target],
            dst_ref=in_strip.at[unit, pair, source],
            send_sem=strip_sent.at[unit, pair, target],
            recv_sem=strip_here.at[unit, pair, source],
            **at(target, g),
        )

    def own_strip(unit, pair):
        return pltpu.make_async_copy(
            out_strip.at[unit, pair, me], in_strip.at[unit, pair, me], strip_own.at[unit, pair]
        )

    def weight(target, source):
        return pltpu.make_async_remote_copy(
            src_ref=weight_ref,
            dst_ref=all_weights.at[source],
            send_sem=weight_sent.at[target],
            recv_sem=weight_here.at[source],
            **at(target, g),
        )

    def block(u, target, source):
        return pltpu.make_async_remote_copy(
            src_ref=out_block.at[u, target],
            dst_ref=y_ref.at[1 - u, source + u],
            send_sem=block_sent.at[u, target],
            recv_sem=block_here.at[u, source],
            **at(target, g),
        )

    def halo(u, source):
        return pltpu.make_async_remote_copy(
            src_ref=y_ref.at[1 - u, source + u],
            dst_ref=y_ref.at[1 - u, source + u + 8],
            send_sem=halo_sent.at[u, source],
            recv_sem=halo_here.at[u, source],
            **at(me, g - 1),
        )

    def edge(u):
        return pltpu.make_async_remote_copy(
            src_ref=y_ref.at[1 - u, (0, 8)[u]],
            dst_ref=y_ref.at[1 - u, (16, 0)[u]],
            send_sem=edge_sent.at[u],
            recv_sem=edge_here.at[u],
            **at(me, (g - 2, g + 1)[u]),
        )

    def turn(pair):
        load(pair).wait()
        for c in range(2):
            for q in range(2):
                turned = echo_ref[q, pair * 2 + c].T.reshape(8, 2, 16, 256)
                for unit in range(2):
                    out_strip[unit, pair, :, q, c] = turned[:, unit]

    def send(unit, pair):
        for k in range(1, 8):
            strip(unit, pair, peer(k), me).start()
        own_strip(unit, pair).start()

    loads[0].wait()
    for half in range(2):
        weight_ref[half] = weights_ref[:, 128 * half : 128 * half + 128]
    turn(0)
    pl.semaphore_wait(barrier, 7 + gates - 1)
    for k in range(1, 8):
        weight(peer(k), me).start()
    send(0, 0)
    for k in range(1, 8):
        pl.semaphore_signal(row_here, inc=1, **at(peer(k), g))

    def turn_and_send(pair, carry):
        turn(pair)
        send(0, pair)
        return carry

    def send_second(pair, carry):
        send(1, pair)
        return carry

    lax.fori_loop(1, PAIRS, turn_and_send, 0)
    lax.fori_loop(0, EARLY, send_second, 0)

    for copy in loads[1:]:
        copy.wait()
    code_ref[...] = slot_codes(track_ref[0], track_ref[1], track_ref[2], code_ref.shape[1])
    move = pltpu.make_async_copy(code_ref, codes_ref, code_moved)
    move.start()
    all_weights[me] = weight_ref[...]
    nothing = jnp.zeros((2 * ROWS, 256), BF16)

    @pl.when(g == 0)
    def _():
        y_ref[0, 0] = nothing

    @pl.when(g == gates - 1)
    def _():
        for k in range(8):
            y_ref[1, 8 + k] = nothing
            y_ref[0, 9 + k] = nothing

    @pl.when(g >= gates - 2)
    def _():
        y_ref[1, 16] = nothing

    make_taps(replica_ref, taps_ref)
    for k in range(1, 8):
        weight(me, peer(k)).wait_recv()

    def widen_step(i, carry):
        widen(i, all_weights, wide_ref)
        return carry

    lax.fori_loop(0, 32, widen_step, 0)
    move.wait()

    def transform(u, first, last):
        def one(pair, carry):
            own_strip(u, pair).wait()
            for k in range(1, 8):
                strip(u, pair, me, peer(k)).wait_recv()
            doppler_pair(
                pair, in_strip.at[u, pair], wide_ref, dft_ref, twist_ref, z_ref, acc_ref
            )
            return carry

        lax.fori_loop(first, last, one, 0)

    def send_blocks(u):
        for j in range(8):

            @pl.when(me == j)
            def _():
                pack_block(j, acc_ref, y_ref.at[1 - u, j + u])

            @pl.when(me != j)
            def _():
                pack_block(j, acc_ref, out_block.at[u, j])
                block(u, j, me).start()

    def pass_on(u, source):
        @pl.when(g > 0)
        def _():
            halo(u, source).start()

        if u == 0:

            @pl.when((source == 0) & (g > 1))
            def _():
                edge(0).start()

        else:

            @pl.when((source == 7) & (g < gates - 1))
            def _():
                edge(1).start()

    def pass_all(u):
        pass_on(u, me)

        def arrive(k, carry):
            source = peer(k)
            block(u, me, source).wait_recv()
            pass_on(u, source)
            return carry

        lax.fori_loop(1, 8, arrive, 0)

    def compress_unit(u):
        @pl.when(g < gates - 1)
        def _():
            for source in range(8):
                halo(u, source).wait_recv()

        @pl.when((g < gates - 2, g > 0)[u])
        def _():
            edge(u).wait_recv()

        compress(1 - u, y_ref, taps_ref, sum_ref)

    acc_ref[...] = jnp.zeros_like(acc_ref)
    transform(0, 0, PAIRS)
    send_blocks(0)
    acc_ref[...] = jnp.zeros_like(acc_ref)
    transform(1, 0, PAIRS)
    send_blocks(1)
    pass_all(0)
    pass_all(1)
    compress_unit(0)
    compress_unit(1)
    frame(g == 0, sum_ref, frame_ref.reshape(33 * UNITS * 8, 128))

    pl.semaphore_wait(row_here, 7)
    devices = 8 * gates
    here = me * gates + g

    def cut_block(owner):
        tiles = []
        for slot in range(5):
            code = codes_ref[0, owner * 5 + slot]
            base = jnp.clip(lax.shift_right_logical(code, 8), 0, 32 * UNITS - 2)
            tile = cut(base, code & 127, frame_ref)
            tiles.append(jnp.where(code & 128 != 0, tile, 0.0))
        return jnp.concatenate(tiles, axis=0).astype(BF16)

    def tile(owner, holder):
        return pltpu.make_async_remote_copy(
            src_ref=out_tile.at[owner],
            dst_ref=tiles_ref.at[holder],
            send_sem=tile_sent,
            recv_sem=tile_here,
            **at(owner // gates, lax.rem(owner, gates)),
        )

    def cut_and_send(step, carry):
        near = [lax.rem(here + 1 + step * STEP + k, devices) for k in range(STEP)]
        for owner, part in zip(near, [cut_block(owner) for owner in near]):
            out_tile[owner] = part
        for owner in near:
            tile(owner, here).start()
        return carry

    steps = (devices - 1) // STEP
    lax.fori_loop(0, steps, cut_and_send, 0)
    for k in range(1 + steps * STEP, devices):
        owner = lax.rem(here + k, devices)
        out_tile[owner] = cut_block(owner)
        tile(owner, here).start()
    tiles_ref[here] = cut_block(here)

    for u in range(2):

        @pl.when(g > 0)
        def _():
            for source in range(8):
                halo(u, source).wait_send()

        @pl.when((g > 1, g < gates - 1)[u])
        def _():
            edge(u).wait_send()

    for k in range(1, 8):
        weight(peer(k), me).wait_send()
        for u in range(2):
            block(u, peer(k), me).wait_send()

    def sent(pair, carry):
        for k in range(1, 8):
            for u in range(2):
                strip(u, pair, peer(k), me).wait_send()
        return carry

    lax.fori_loop(0, PAIRS, sent, 0)
    everyone = pltpu.make_async_remote_copy(
        src_ref=out_tile.at[pl.ds(0, devices - 1)],
        dst_ref=tiles_ref.at[pl.ds(0, devices - 1)],
        send_sem=tile_sent,
        recv_sem=tile_here,
        **at(me, g),
    )
    everyone.wait_recv()
    everyone.wait_send()


def tiles(echoes, weights, replica, doppler, gate, owner, owners):
    dft, twist = tables()
    dma = pltpu.SemaphoreType.DMA
    hbm = pl.BlockSpec(memory_space=pltpu.HBM)
    return pl.pallas_call(
        tiles_kernel,
        out_shape=jax.ShapeDtypeStruct((owners, ROWS, 128), BF16),
        in_specs=[hbm] * 8,
        out_specs=VMEM,
        scratch_shapes=[
            pltpu.VMEM((2, 8, 256, 256), BF16),
            pltpu.VMEM((32, 256), F32),
            pltpu.VMEM((2, 256), BF16),
            pltpu.VMEM((512, 512), BF16),
            pltpu.VMEM((2, 8, 256), F32),
            pltpu.VMEM((3, 1, 256), jnp.int32),
            pltpu.VMEM((1, owners * 5), jnp.int32),
            pltpu.SMEM((1, owners * 5), jnp.int32),
            pltpu.VMEM((2, 32, 128), F32),
            pltpu.VMEM((33 * UNITS, 8, 128), F32),
            pltpu.VMEM((owners, ROWS, 128), BF16),
            pltpu.VMEM((2, PAIRS, 8, 2, 2, 16, 256), BF16),
            pltpu.VMEM((2, PAIRS, 8, 2, 2, 16, 256), BF16),
            pltpu.VMEM((8, 2, 32, 128), F32),
            pltpu.VMEM((32, 256, 128), F32),
            pltpu.VMEM((256, 512), BF16),
            pltpu.VMEM((2, 2, 272, 128), F32),
            pltpu.VMEM((2, 8, 2 * ROWS, 256), BF16),
            pltpu.VMEM((2, 17, 2 * ROWS, 256), BF16),
            pltpu.VMEM((17, 256, 256), BF16),
            pltpu.VMEM((2, UNITS * ROWS, 256), F32),
            dma((2, PAIRS, 8)),
            dma((2, PAIRS, 8)),
            dma((2, PAIRS)),
            dma((8,)),
            dma((8,)),
            dma((2, 8)),
            dma((2, 8)),
            dma((2, 8)),
            dma((2, 8)),
            dma((2,)),
            dma((2,)),
            dma((PAIRS,)),
            dma((7,)),
            dma(()),
            dma(()),
            dma(()),
            pltpu.SemaphoreType.REGULAR,
        ],
        compiler_params=params(60, collective_id=0, has_side_effects=True),
        cost_estimate=pl.CostEstimate(flops=6 * 10**9, bytes_accessed=8 << 20, transcendentals=0),
    )(echoes, weights, replica, jnp.asarray(dft), jnp.asarray(twist), doppler, gate, owner)


def rows_kernel(tiles_ref, out_ref, in_ref):
    slots = out_ref.shape[0]
    in_ref[...] = tiles_ref[...].reshape(8 * slots, 128).astype(F32)
    for k in range(8):
        out_ref[:, 128 * k : 128 * k + 128] = in_ref[pl.ds(k, slots, stride=8), :]


def params(mib, **more):
    return pltpu.CompilerParams(vmem_limit_bytes=mib << 20, **more)


def local(echoes, replica, beam_weights, track_doppler, track_gate, track_owner):
    pulse_devices, gate_devices = lax.axis_size("pulse"), lax.axis_size("gate")
    owners = pulse_devices * gate_devices
    tracks = track_owner.shape[0]
    capacity = 5
    rows = (x.reshape(1, tracks) for x in (track_doppler, track_gate, track_owner))
    received = tiles(echoes, beam_weights.reshape(32, 256), replica, *rows, owners)
    return pl.pallas_call(
        rows_kernel,
        out_shape=jax.ShapeDtypeStruct((owners * capacity, 1024), F32),
        in_specs=[VMEM],
        out_specs=VMEM,
        scratch_shapes=[pltpu.VMEM((owners * capacity * 8, 128), F32)],
        compiler_params=params(16),
    )(received)


def solution(mesh):
    return jax.shard_map(
        local,
        mesh=mesh,
        in_specs=(
            P(None, None, "pulse", "gate"),
            P(),
            P(None, None, None, "pulse"),
            P(("pulse", "gate")),
            P(("pulse", "gate")),
            P(("pulse", "gate")),
        ),
        out_specs=P(("pulse", "gate"), None),
        check_vma=False,
    )
```

```python
import functools
import math

import jax
import jax.numpy as jnp
import numpy as np
from jax import lax
from jax.experimental import pallas as pl
from jax.experimental.pallas import tpu as pltpu
from jax.sharding import PartitionSpec as P

F32 = jnp.float32
BF16 = jnp.bfloat16
UNITS = 18
ROWS = 40
VMEM = pl.BlockSpec(memory_space=pltpu.VMEM)
SMEM = pl.BlockSpec(memory_space=pltpu.SMEM)


def tables():
    angle = 2.0 * np.pi * ((np.arange(256)[:, None] * np.arange(256)[None, :]) % 256) / 256.0
    cos, sin = np.cos(angle), np.sin(angle)
    dft = np.block([[cos, sin], [-sin, cos]]).astype(jnp.bfloat16)
    twist = 2.0 * np.pi * (np.arange(8)[:, None] * np.arange(256)[None, :]) / 2048.0
    scale = 1.0 / 1024.0
    return dft, np.stack([np.cos(twist) * scale, np.sin(twist) * scale]).astype(np.float32)


def cadd(a, b):
    return (a[0] + b[0], a[1] + b[1])


def csub(a, b):
    return (a[0] - b[0], a[1] - b[1])


def turn(a):
    return (a[1], -a[0])


def dft4(a):
    e0, e1 = cadd(a[0], a[2]), csub(a[0], a[2])
    f0, f1 = cadd(a[1], a[3]), turn(csub(a[1], a[3]))
    return [cadd(e0, f0), cadd(e1, f1), csub(e0, f0), csub(e1, f1)]


def dft8(x):
    root = math.sqrt(0.5)
    even = dft4([cadd(x[k], x[k + 4]) for k in range(4)])
    b = [csub(x[k], x[k + 4]) for k in range(4)]
    b1 = ((b[1][0] + b[1][1]) * root, (b[1][1] - b[1][0]) * root)
    b3 = ((b[3][1] - b[3][0]) * root, (b[3][0] + b[3][1]) * -root)
    odd = dft4([b[0], b1, turn(b[2]), b3])
    return [(even, odd)[d % 2][d // 2] for d in range(8)]


def doppler_pair(pair, x_ref, wide_ref, dft_ref, twist_ref, z_ref, acc_ref):
    for c in range(2):
        for half in range(2):
            cols = slice(128 * half, 128 * half + 128)
            x = [tuple(x_ref[pb, q, c, :, cols].astype(F32) for q in range(2)) for pb in range(8)]
            for d, (re, im) in enumerate(dft8(x)):
                cos, sin = (twist_ref[k, d : d + 1, cols] for k in range(2))
                at = slice(128 * c + 16 * d, 128 * c + 16 * d + 16)
                z_ref[at, 128 * half : 128 * half + 128] = (re * cos + im * sin).astype(BF16)
                z_ref[at, 256 + 128 * half : 384 + 128 * half] = (im * cos - re * sin).astype(BF16)
    spec = lax.dot_general(
        dft_ref[...], z_ref[...], (((1,), (1,)), ((), ())), preferred_element_type=F32
    )
    for b in range(2):
        real, imag = 0.0, 0.0
        for c in range(2):
            w_re, w_im = (wide_ref[(q * 2 + b) * 8 + 2 * pair + c] for q in range(2))
            cols = slice(128 * c, 128 * c + 128)
            re, im = spec[:256, cols], spec[256:, cols]
            real += w_re * re - w_im * im
            imag += w_re * im + w_im * re
        acc_ref[0, b, 8:264] += real
        acc_ref[1, b, 8:264] += imag


def widen(i, weight_ref, wide_ref):
    lane = lax.broadcasted_iota(jnp.int32, (16, 128), 1)
    keep = lane // 8 == lax.broadcasted_iota(jnp.int32, (16, 128), 0)
    spread = (
        lax.broadcasted_iota(jnp.int32, (128, 128), 0) % 8
        == lax.broadcasted_iota(jnp.int32, (128, 128), 1) // 16
    )
    spread = jnp.where(spread, 1.0, 0.0).astype(BF16)
    w = jnp.concatenate(
        [
            jnp.where(keep, weight_ref[source, half, pl.ds(i, 1), :], 0.0)
            for source in range(8)
            for half in range(2)
        ],
        axis=0,
    )
    high = w.astype(BF16)
    rest = w - high.astype(F32)
    mid = rest.astype(BF16)
    low = (rest - mid.astype(F32)).astype(BF16)
    wide_ref[i] = sum(jnp.dot(part, spread, preferred_element_type=F32) for part in (low, mid, high))


def pack_block(j, acc_ref, out_ref):
    for q in range(2):
        both = jnp.concatenate(
            [acc_ref[q, b, 32 * j + 7 : 32 * j + 7 + ROWS] for b in range(2)], axis=0
        )
        out_ref[:, 128 * q : 128 * q + 128] = both.astype(BF16)


def make_taps(replica_ref, taps_ref):
    period = (
        lax.broadcasted_iota(jnp.int32, (16, 128), 0)
        == lax.broadcasted_iota(jnp.int32, (16, 128), 1) % 16
    )
    period = jnp.where(period, 1.0, 0.0).astype(F32)
    tables = []
    for q in range(2):
        row = jnp.concatenate(
            [replica_ref[q : q + 1, :].astype(F32), jnp.zeros((1, 128), F32)], axis=1
        )
        shifted = pltpu.roll(jnp.broadcast_to(row, (16, 384)), 0, 1, stride=1, stride_axis=0)
        tables.append(
            lax.dot_general(
                shifted.astype(BF16),
                period.astype(BF16),
                (((0,), (0,)), ((), ())),
                preferred_element_type=F32,
            )
        )
    lane = lax.broadcasted_iota(jnp.int32, (16, 128), 1) // 16
    for j in range(17):
        real, imag = (t[16 * j : 16 * j + 16] for t in tables)
        for d in range(8):
            keep = lane == d
            re, im = jnp.where(keep, real, 0.0), jnp.where(keep, imag, 0.0)
            from_real = jnp.concatenate([re, -im], axis=1).astype(BF16)
            from_imag = jnp.concatenate([im, re], axis=1).astype(BF16)
            taps_ref[j, 16 * d : 16 * d + 16, :] = from_real
            taps_ref[j, 128 + 16 * d : 144 + 16 * d, :] = from_imag


def compress(parity, y_ref, taps_ref, sum_ref):
    half, depth = UNITS // 2, 2 * ROWS
    for out in range(2):
        odd = (parity - out) % 2
        skip = out * (1 - parity)
        total = 9 - odd

        def part(first, count):
            x = jnp.concatenate(
                [
                    y_ref[parity, pl.ds(skip + first + k, half)].reshape(half * depth, 256)
                    for k in range(count)
                ],
                axis=1,
            )
            w = jnp.concatenate([taps_ref[odd + 2 * (first + k)] for k in range(count)], axis=0)
            return jnp.dot(x, w, preferred_element_type=F32)

        for first in range(0, 8, 4):
            count = 5 if first == 4 and total == 9 else 4
            if parity == 1 and first == 0:
                sum_ref[out] = part(first, count)
            else:
                sum_ref[out] += part(first, count)


def frame(first_block, sum_ref, frame_ref):
    for unit in range(UNITS):
        for q in range(2):
            for b in range(2):
                for half in range(2):
                    start = (unit // 2 * 2 + b) * ROWS + half
                    value = sum_ref[unit % 2, start : start + 33, 128 * q : 128 * q + 128]
                    if unit == 0:
                        value = jnp.where(first_block, 0.0, value)
                    at = pl.ds(unit * 8 + q * 4 + b * 2 + half, 33, stride=8 * UNITS)
                    frame_ref[at, :] = value


def slot_codes(doppler, gate, owner, slots):
    row, col = doppler & 255, (gate & 255) + 8
    base = lax.shift_right_logical(row, 3) * UNITS + lax.shift_right_logical(col, 4)
    code = (base * 256 + 128 + (row & 7) * 16 + (col & 15)).astype(F32)
    owner = owner.astype(F32)
    tracks = owner.shape[1]
    column = jnp.broadcast_to(owner, (8, tracks)).T[:, :1]
    square = (tracks, tracks)
    before = lax.broadcasted_iota(jnp.int32, square, 0) < lax.broadcasted_iota(jnp.int32, square, 1)
    same = jnp.where((column == owner) & before, 1.0, 0.0)
    slot = owner * 5.0 + jnp.sum(same, axis=0, keepdims=True)
    both = jnp.concatenate([slot, code, jnp.zeros((6, tracks), F32)], axis=0).T
    place = lax.broadcasted_iota(jnp.int32, (tracks, slots), 1).astype(F32)
    found = jnp.where(both[:, :1] == place, both[:, 1:2], 0.0)
    return jnp.sum(found, axis=0, keepdims=True).astype(jnp.int32)


def cut(base, shift, frame_ref):
    lane = lax.broadcasted_iota(jnp.int32, (8, 128), 1)
    gate = lane & 15
    gate_shift = shift & 15
    near_row, near_gate = lane >= shift - gate_shift, gate >= gate_shift
    f = [frame_ref[base + step] for step in (0, 1, UNITS, UNITS + 1)]
    z = jnp.where(
        near_row, jnp.where(near_gate, f[0], f[1]), jnp.where(near_gate, f[2], f[3])
    )
    return jnp.where(
        gate < 16 - gate_shift,
        pltpu.roll(z, (128 - shift) & 127, 1),
        pltpu.roll(z, (144 - shift) & 127, 1),
    )


PAIRS = 4
EARLY = 4
STEP = 3


def tiles_kernel(
    echo_hbm,
    weights_hbm,
    replica_hbm,
    dft_hbm,
    twist_hbm,
    doppler_hbm,
    gate_hbm,
    owner_hbm,
    tiles_ref,
    echo_ref,
    weights_ref,
    replica_ref,
    dft_ref,
    twist_ref,
    track_ref,
    code_ref,
    codes_ref,
    weight_ref,
    frame_ref,
    out_tile,
    out_strip,
    in_strip,
    all_weights,
    wide_ref,
    z_ref,
    acc_ref,
    out_block,
    y_ref,
    taps_ref,
    sum_ref,
    strip_sent,
    strip_here,
    strip_own,
    weight_sent,
    weight_here,
    block_sent,
    block_here,
    halo_sent,
    halo_here,
    edge_sent,
    edge_here,
    echo_loaded,
    loaded,
    code_moved,
    tile_sent,
    tile_here,
    row_here,
):
    me, g = lax.axis_index("pulse"), lax.axis_index("gate")
    gates = lax.axis_size("gate")
    barrier = pltpu.get_barrier_semaphore()

    def at(pulse, gate):
        return dict(device_id=(pulse, gate), device_id_type=pl.DeviceIdType.MESH)

    def peer(k):
        return lax.rem(me + k, 8)

    def load(pair):
        channels = pl.ds(pair * 2, 2)
        return pltpu.make_async_copy(
            echo_hbm.at[:, channels], echo_ref.at[:, channels], echo_loaded.at[pair]
        )

    small = [
        (weights_hbm, weights_ref),
        (replica_hbm, replica_ref),
        (dft_hbm, dft_ref),
        (twist_hbm, twist_ref),
        (doppler_hbm, track_ref.at[0]),
        (gate_hbm, track_ref.at[1]),
        (owner_hbm, track_ref.at[2]),
    ]
    loads = [
        pltpu.make_async_copy(source, target, loaded.at[k])
        for k, (source, target) in enumerate(small)
    ]
    for k in range(1, 8):
        pl.semaphore_signal(barrier, inc=1, **at(peer(k), g))
    for k in range(1, gates):
        pl.semaphore_signal(barrier, inc=1, **at(me, lax.rem(g + k, gates)))
    for pair in range(PAIRS):
        load(pair).start()
    for copy in loads:
        copy.start()

    def strip(unit, pair, target, source):
        return pltpu.make_async_remote_copy(
            src_ref=out_strip.at[unit, pair, target],
            dst_ref=in_strip.at[unit, pair, source],
            send_sem=strip_sent.at[unit, pair, target],
            recv_sem=strip_here.at[unit, pair, source],
            **at(target, g),
        )

    def own_strip(unit, pair):
        return pltpu.make_async_copy(
            out_strip.at[unit, pair, me], in_strip.at[unit, pair, me], strip_own.at[unit, pair]
        )

    def weight(target, source):
        return pltpu.make_async_remote_copy(
            src_ref=weight_ref,
            dst_ref=all_weights.at[source],
            send_sem=weight_sent.at[target],
            recv_sem=weight_here.at[source],
            **at(target, g),
        )

    def block(u, target, source):
        return pltpu.make_async_remote_copy(
            src_ref=out_block.at[u, target],
            dst_ref=y_ref.at[1 - u, source + u],
            send_sem=block_sent.at[u, target],
            recv_sem=block_here.at[u, source],
            **at(target, g),
        )

    def halo(u, source):
        return pltpu.make_async_remote_copy(
            src_ref=y_ref.at[1 - u, source + u],
            dst_ref=y_ref.at[1 - u, source + u + 8],
            send_sem=halo_sent.at[u, source],
            recv_sem=halo_here.at[u, source],
            **at(me, g - 1),
        )

    def edge(u):
        return pltpu.make_async_remote_copy(
            src_ref=y_ref.at[1 - u, (0, 8)[u]],
            dst_ref=y_ref.at[1 - u, (16, 0)[u]],
            send_sem=edge_sent.at[u],
            recv_sem=edge_here.at[u],
            **at(me, (g - 2, g + 1)[u]),
        )

    def turn(pair):
        load(pair).wait()
        for c in range(2):
            for q in range(2):
                turned = echo_ref[q, pair * 2 + c].T.reshape(8, 2, 16, 256)
                for unit in range(2):
                    out_strip[unit, pair, :, q, c] = turned[:, unit]

    def send(unit, pair):
        for k in range(1, 8):
            strip(unit, pair, peer(k), me).start()
        own_strip(unit, pair).start()

    loads[0].wait()
    for half in range(2):
        weight_ref[half] = weights_ref[:, 128 * half : 128 * half + 128]
    turn(0)
    pl.semaphore_wait(barrier, 7 + gates - 1)
    for k in range(1, 8):
        weight(peer(k), me).start()
    send(0, 0)
    for k in range(1, 8):
        pl.semaphore_signal(row_here, inc=1, **at(peer(k), g))

    def turn_and_send(pair, carry):
        turn(pair)
        send(0, pair)
        return carry

    def send_second(pair, carry):
        send(1, pair)
        return carry

    lax.fori_loop(1, PAIRS, turn_and_send, 0)
    lax.fori_loop(0, EARLY, send_second, 0)

    for copy in loads[1:]:
        copy.wait()
    code_ref[...] = slot_codes(track_ref[0], track_ref[1], track_ref[2], code_ref.shape[1])
    move = pltpu.make_async_copy(code_ref, codes_ref, code_moved)
    move.start()
    all_weights[me] = weight_ref[...]
    nothing = jnp.zeros((2 * ROWS, 256), BF16)

    @pl.when(g == 0)
    def _():
        y_ref[0, 0] = nothing

    @pl.when(g == gates - 1)
    def _():
        for k in range(8):
            y_ref[1, 8 + k] = nothing
            y_ref[0, 9 + k] = nothing

    @pl.when(g >= gates - 2)
    def _():
        y_ref[1, 16] = nothing

    make_taps(replica_ref, taps_ref)
    for k in range(1, 8):
        weight(me, peer(k)).wait_recv()

    def widen_step(i, carry):
        widen(i, all_weights, wide_ref)
        return carry

    lax.fori_loop(0, 32, widen_step, 0)
    move.wait()

    def transform(u, first, last):
        def one(pair, carry):
            own_strip(u, pair).wait()
            for k in range(1, 8):
                strip(u, pair, me, peer(k)).wait_recv()
            doppler_pair(
                pair, in_strip.at[u, pair], wide_ref, dft_ref, twist_ref, z_ref, acc_ref
            )
            return carry

        lax.fori_loop(first, last, one, 0)

    def send_blocks(u):
        for j in range(8):

            @pl.when(me == j)
            def _():
                pack_block(j, acc_ref, y_ref.at[1 - u, j + u])

            @pl.when(me != j)
            def _():
                pack_block(j, acc_ref, out_block.at[u, j])
                block(u, j, me).start()

    def pass_on(u, source):
        @pl.when(g > 0)
        def _():
            halo(u, source).start()

        if u == 0:

            @pl.when((source == 0) & (g > 1))
            def _():
                edge(0).start()

        else:

            @pl.when((source == 7) & (g < gates - 1))
            def _():
                edge(1).start()

    def pass_all(u):
        pass_on(u, me)

        def arrive(k, carry):
            source = peer(k)
            block(u, me, source).wait_recv()
            pass_on(u, source)
            return carry

        lax.fori_loop(1, 8, arrive, 0)

    def compress_unit(u):
        @pl.when(g < gates - 1)
        def _():
            for source in range(8):
                halo(u, source).wait_recv()

        @pl.when((g < gates - 2, g > 0)[u])
        def _():
            edge(u).wait_recv()

        compress(1 - u, y_ref, taps_ref, sum_ref)

    acc_ref[...] = jnp.zeros_like(acc_ref)
    transform(0, 0, PAIRS)
    send_blocks(0)
    acc_ref[...] = jnp.zeros_like(acc_ref)
    transform(1, 0, PAIRS)
    send_blocks(1)
    pass_all(0)
    pass_all(1)
    compress_unit(0)
    compress_unit(1)
    frame(g == 0, sum_ref, frame_ref.reshape(33 * UNITS * 8, 128))

    pl.semaphore_wait(row_here, 7)
    devices = 8 * gates
    here = me * gates + g

    def cut_block(owner):
        tiles = []
        for slot in range(5):
            code = codes_ref[0, owner * 5 + slot]
            base = jnp.clip(lax.shift_right_logical(code, 8), 0, 32 * UNITS - 2)
            tile = cut(base, code & 127, frame_ref)
            tiles.append(jnp.where(code & 128 != 0, tile, 0.0))
        return jnp.concatenate(tiles, axis=0).astype(BF16)

    def tile(owner, holder):
        return pltpu.make_async_remote_copy(
            src_ref=out_tile.at[owner],
            dst_ref=tiles_ref.at[holder],
            send_sem=tile_sent,
            recv_sem=tile_here,
            **at(owner // gates, lax.rem(owner, gates)),
        )

    def cut_and_send(step, carry):
        near = [lax.rem(here + 1 + step * STEP + k, devices) for k in range(STEP)]
        for owner, part in zip(near, [cut_block(owner) for owner in near]):
            out_tile[owner] = part
        for owner in near:
            tile(owner, here).start()
        return carry

    steps = (devices - 1) // STEP
    lax.fori_loop(0, steps, cut_and_send, 0)
    for k in range(1 + steps * STEP, devices):
        owner = lax.rem(here + k, devices)
        out_tile[owner] = cut_block(owner)
        tile(owner, here).start()
    tiles_ref[here] = cut_block(here)

    for u in range(2):

        @pl.when(g > 0)
        def _():
            for source in range(8):
                halo(u, source).wait_send()

        @pl.when((g > 1, g < gates - 1)[u])
        def _():
            edge(u).wait_send()

    for k in range(1, 8):
        weight(peer(k), me).wait_send()
        for u in range(2):
            block(u, peer(k), me).wait_send()

    def sent(pair, carry):
        for k in range(1, 8):
            for u in range(2):
                strip(u, pair, peer(k), me).wait_send()
        return carry

    lax.fori_loop(0, PAIRS, sent, 0)
    everyone = pltpu.make_async_remote_copy(
        src_ref=out_tile.at[pl.ds(0, devices - 1)],
        dst_ref=tiles_ref.at[pl.ds(0, devices - 1)],
        send_sem=tile_sent,
        recv_sem=tile_here,
        **at(me, g),
    )
    everyone.wait_recv()
    everyone.wait_send()


def tiles(echoes, weights, replica, doppler, gate, owner, owners):
    dft, twist = tables()
    dma = pltpu.SemaphoreType.DMA
    hbm = pl.BlockSpec(memory_space=pltpu.HBM)
    return pl.pallas_call(
        tiles_kernel,
        out_shape=jax.ShapeDtypeStruct((owners, ROWS, 128), BF16),
        in_specs=[hbm] * 8,
        out_specs=VMEM,
        scratch_shapes=[
            pltpu.VMEM((2, 8, 256, 256), BF16),
            pltpu.VMEM((32, 256), F32),
            pltpu.VMEM((2, 256), BF16),
            pltpu.VMEM((512, 512), BF16),
            pltpu.VMEM((2, 8, 256), F32),
            pltpu.VMEM((3, 1, 256), jnp.int32),
            pltpu.VMEM((1, owners * 5), jnp.int32),
            pltpu.SMEM((1, owners * 5), jnp.int32),
            pltpu.VMEM((2, 32, 128), F32),
            pltpu.VMEM((33 * UNITS, 8, 128), F32),
            pltpu.VMEM((owners, ROWS, 128), BF16),
            pltpu.VMEM((2, PAIRS, 8, 2, 2, 16, 256), BF16),
            pltpu.VMEM((2, PAIRS, 8, 2, 2, 16, 256), BF16),
            pltpu.VMEM((8, 2, 32, 128), F32),
            pltpu.VMEM((32, 256, 128), F32),
            pltpu.VMEM((256, 512), BF16),
            pltpu.VMEM((2, 2, 272, 128), F32),
            pltpu.VMEM((2, 8, 2 * ROWS, 256), BF16),
            pltpu.VMEM((2, 17, 2 * ROWS, 256), BF16),
            pltpu.VMEM((17, 256, 256), BF16),
            pltpu.VMEM((2, UNITS * ROWS, 256), F32),
            dma((2, PAIRS, 8)),
            dma((2, PAIRS, 8)),
            dma((2, PAIRS)),
            dma((8,)),
            dma((8,)),
            dma((2, 8)),
            dma((2, 8)),
            dma((2, 8)),
            dma((2, 8)),
            dma((2,)),
            dma((2,)),
            dma((PAIRS,)),
            dma((7,)),
            dma(()),
            dma(()),
            dma(()),
            pltpu.SemaphoreType.REGULAR,
        ],
        compiler_params=params(60, collective_id=0, has_side_effects=True),
        cost_estimate=pl.CostEstimate(flops=6 * 10**9, bytes_accessed=8 << 20, transcendentals=0),
    )(echoes, weights, replica, jnp.asarray(dft), jnp.asarray(twist), doppler, gate, owner)


PARTS = 4


def rows_kernel(tiles_hbm, out_hbm, tiles_ref, wide_ref, out_ref, here, gone):
    holders, slots = tiles_ref.shape[1], out_ref.shape[1]
    loads = [
        pltpu.make_async_copy(
            tiles_hbm.at[pl.ds(part * holders, holders)], tiles_ref.at[part], here.at[part]
        )
        for part in range(PARTS)
    ]
    stores = [
        pltpu.make_async_copy(
            out_ref.at[part], out_hbm.at[pl.ds(part * slots, slots)], gone.at[part]
        )
        for part in range(PARTS)
    ]
    for load in loads:
        load.start()
    for part in range(PARTS):
        loads[part].wait()
        wide_ref[part] = tiles_ref[part].reshape(8 * slots, 128).astype(F32)
        for k in range(8):
            rows = wide_ref[part, pl.ds(k, slots, stride=8), :]
            out_ref[part, :, 128 * k : 128 * k + 128] = rows
        stores[part].start()
    for store in stores:
        store.wait()


def params(mib, **more):
    return pltpu.CompilerParams(vmem_limit_bytes=mib << 20, **more)


def local(echoes, replica, beam_weights, track_doppler, track_gate, track_owner):
    pulse_devices, gate_devices = lax.axis_size("pulse"), lax.axis_size("gate")
    owners = pulse_devices * gate_devices
    tracks = track_owner.shape[0]
    capacity = 5
    rows = (x.reshape(1, tracks) for x in (track_doppler, track_gate, track_owner))
    received = tiles(echoes, beam_weights.reshape(32, 256), replica, *rows, owners)
    hbm = pl.BlockSpec(memory_space=pltpu.HBM)
    slots = owners * capacity // PARTS
    return pl.pallas_call(
        rows_kernel,
        out_shape=jax.ShapeDtypeStruct((owners * capacity, 1024), F32),
        in_specs=[hbm],
        out_specs=hbm,
        scratch_shapes=[
            pltpu.VMEM((PARTS, owners // PARTS, capacity * 8, 128), BF16),
            pltpu.VMEM((PARTS, slots * 8, 128), F32),
            pltpu.VMEM((PARTS, slots, 1024), F32),
            pltpu.SemaphoreType.DMA((PARTS,)),
            pltpu.SemaphoreType.DMA((PARTS,)),
        ],
        compiler_params=params(60),
    )(received)


def solution(mesh):
    return jax.shard_map(
        local,
        mesh=mesh,
        in_specs=(
            P(None, None, "pulse", "gate"),
            P(),
            P(None, None, None, "pulse"),
            P(("pulse", "gate")),
            P(("pulse", "gate")),
            P(("pulse", "gate")),
        ),
        out_specs=P(("pulse", "gate"), None),
        check_vma=False,
    )
```

```python
import functools
import math

import jax
import jax.numpy as jnp
import numpy as np
from jax import lax
from jax.experimental import pallas as pl
from jax.experimental.pallas import tpu as pltpu
from jax.sharding import PartitionSpec as P

F32 = jnp.float32
BF16 = jnp.bfloat16
UNITS = 18
ROWS = 40
VMEM = pl.BlockSpec(memory_space=pltpu.VMEM)
SMEM = pl.BlockSpec(memory_space=pltpu.SMEM)


def tables():
    angle = 2.0 * np.pi * ((np.arange(256)[:, None] * np.arange(256)[None, :]) % 256) / 256.0
    cos, sin = np.cos(angle), np.sin(angle)
    dft = np.block([[cos, sin], [-sin, cos]]).astype(jnp.bfloat16)
    twist = 2.0 * np.pi * (np.arange(8)[:, None] * np.arange(256)[None, :]) / 2048.0
    scale = 1.0 / 1024.0
    return dft, np.stack([np.cos(twist) * scale, np.sin(twist) * scale]).astype(np.float32)


def cadd(a, b):
    return (a[0] + b[0], a[1] + b[1])


def csub(a, b):
    return (a[0] - b[0], a[1] - b[1])


def turn(a):
    return (a[1], -a[0])


def dft4(a):
    e0, e1 = cadd(a[0], a[2]), csub(a[0], a[2])
    f0, f1 = cadd(a[1], a[3]), turn(csub(a[1], a[3]))
    return [cadd(e0, f0), cadd(e1, f1), csub(e0, f0), csub(e1, f1)]


def dft8(x):
    root = math.sqrt(0.5)
    even = dft4([cadd(x[k], x[k + 4]) for k in range(4)])
    b = [csub(x[k], x[k + 4]) for k in range(4)]
    b1 = ((b[1][0] + b[1][1]) * root, (b[1][1] - b[1][0]) * root)
    b3 = ((b[3][1] - b[3][0]) * root, (b[3][0] + b[3][1]) * -root)
    odd = dft4([b[0], b1, turn(b[2]), b3])
    return [(even, odd)[d % 2][d // 2] for d in range(8)]


def doppler_pair(pair, x_ref, wide_ref, dft_ref, twist_ref, z_ref, acc_ref):
    for c in range(2):
        for half in range(2):
            cols = slice(128 * half, 128 * half + 128)
            x = [tuple(x_ref[pb, q, c, :, cols].astype(F32) for q in range(2)) for pb in range(8)]
            for d, (re, im) in enumerate(dft8(x)):
                cos, sin = (twist_ref[k, d : d + 1, cols] for k in range(2))
                at = slice(128 * c + 16 * d, 128 * c + 16 * d + 16)
                z_ref[at, 128 * half : 128 * half + 128] = (re * cos + im * sin).astype(BF16)
                z_ref[at, 256 + 128 * half : 384 + 128 * half] = (im * cos - re * sin).astype(BF16)
    spec = lax.dot_general(
        dft_ref[...], z_ref[...], (((1,), (1,)), ((), ())), preferred_element_type=F32
    )
    for b in range(2):
        real, imag = 0.0, 0.0
        for c in range(2):
            w_re, w_im = (wide_ref[(q * 2 + b) * 8 + 2 * pair + c] for q in range(2))
            cols = slice(128 * c, 128 * c + 128)
            re, im = spec[:256, cols], spec[256:, cols]
            real += w_re * re - w_im * im
            imag += w_re * im + w_im * re
        acc_ref[0, b, 8:264] += real
        acc_ref[1, b, 8:264] += imag


def widen(i, weight_ref, wide_ref):
    lane = lax.broadcasted_iota(jnp.int32, (16, 128), 1)
    keep = lane // 8 == lax.broadcasted_iota(jnp.int32, (16, 128), 0)
    spread = (
        lax.broadcasted_iota(jnp.int32, (128, 128), 0) % 8
        == lax.broadcasted_iota(jnp.int32, (128, 128), 1) // 16
    )
    spread = jnp.where(spread, 1.0, 0.0).astype(BF16)
    w = jnp.concatenate(
        [
            jnp.where(keep, weight_ref[source, half, pl.ds(i, 1), :], 0.0)
            for source in range(8)
            for half in range(2)
        ],
        axis=0,
    )
    high = w.astype(BF16)
    rest = w - high.astype(F32)
    mid = rest.astype(BF16)
    low = (rest - mid.astype(F32)).astype(BF16)
    wide_ref[i] = sum(jnp.dot(part, spread, preferred_element_type=F32) for part in (low, mid, high))


def pack_block(j, acc_ref, out_ref):
    for q in range(2):
        both = jnp.concatenate(
            [acc_ref[q, b, 32 * j + 7 : 32 * j + 7 + ROWS] for b in range(2)], axis=0
        )
        out_ref[:, 128 * q : 128 * q + 128] = both.astype(BF16)


def make_taps(replica_ref, taps_ref):
    period = (
        lax.broadcasted_iota(jnp.int32, (16, 128), 0)
        == lax.broadcasted_iota(jnp.int32, (16, 128), 1) % 16
    )
    period = jnp.where(period, 1.0, 0.0).astype(F32)
    tables = []
    for q in range(2):
        row = jnp.concatenate(
            [replica_ref[q : q + 1, :].astype(F32), jnp.zeros((1, 128), F32)], axis=1
        )
        shifted = pltpu.roll(jnp.broadcast_to(row, (16, 384)), 0, 1, stride=1, stride_axis=0)
        tables.append(
            lax.dot_general(
                shifted.astype(BF16),
                period.astype(BF16),
                (((0,), (0,)), ((), ())),
                preferred_element_type=F32,
            )
        )
    lane = lax.broadcasted_iota(jnp.int32, (16, 128), 1) // 16
    for j in range(17):
        real, imag = (t[16 * j : 16 * j + 16] for t in tables)
        for d in range(8):
            keep = lane == d
            re, im = jnp.where(keep, real, 0.0), jnp.where(keep, imag, 0.0)
            from_real = jnp.concatenate([re, -im], axis=1).astype(BF16)
            from_imag = jnp.concatenate([im, re], axis=1).astype(BF16)
            taps_ref[j, 16 * d : 16 * d + 16, :] = from_real
            taps_ref[j, 128 + 16 * d : 144 + 16 * d, :] = from_imag


def compress(parity, y_ref, taps_ref, sum_ref):
    half, depth = UNITS // 2, 2 * ROWS
    for out in range(2):
        odd = (parity - out) % 2
        skip = out * (1 - parity)
        total = 9 - odd

        def part(first, count):
            x = jnp.concatenate(
                [
                    y_ref[parity, pl.ds(skip + first + k, half)].reshape(half * depth, 256)
                    for k in range(count)
                ],
                axis=1,
            )
            w = jnp.concatenate([taps_ref[odd + 2 * (first + k)] for k in range(count)], axis=0)
            return jnp.dot(x, w, preferred_element_type=F32)

        for first in range(0, 8, 4):
            count = 5 if first == 4 and total == 9 else 4
            if parity == 1 and first == 0:
                sum_ref[out] = part(first, count)
            else:
                sum_ref[out] += part(first, count)


def frame(first_block, sum_ref, frame_ref):
    for unit in range(UNITS):
        for q in range(2):
            for b in range(2):
                for half in range(2):
                    start = (unit // 2 * 2 + b) * ROWS + half
                    value = sum_ref[unit % 2, start : start + 33, 128 * q : 128 * q + 128]
                    if unit == 0:
                        value = jnp.where(first_block, 0.0, value)
                    at = pl.ds(unit * 8 + q * 4 + b * 2 + half, 33, stride=8 * UNITS)
                    frame_ref[at, :] = value


def slot_codes(doppler, gate, owner, slots):
    row, col = doppler & 255, (gate & 255) + 8
    base = lax.shift_right_logical(row, 3) * UNITS + lax.shift_right_logical(col, 4)
    code = (base * 256 + 128 + (row & 7) * 16 + (col & 15)).astype(F32)
    owner = owner.astype(F32)
    tracks = owner.shape[1]
    column = jnp.broadcast_to(owner, (8, tracks)).T[:, :1]
    square = (tracks, tracks)
    before = lax.broadcasted_iota(jnp.int32, square, 0) < lax.broadcasted_iota(jnp.int32, square, 1)
    same = jnp.where((column == owner) & before, 1.0, 0.0)
    slot = owner * 5.0 + jnp.sum(same, axis=0, keepdims=True)
    both = jnp.concatenate([slot, code, jnp.zeros((6, tracks), F32)], axis=0).T
    place = lax.broadcasted_iota(jnp.int32, (tracks, slots), 1).astype(F32)
    found = jnp.where(both[:, :1] == place, both[:, 1:2], 0.0)
    return jnp.sum(found, axis=0, keepdims=True).astype(jnp.int32)


def cut(base, shift, frame_ref):
    lane = lax.broadcasted_iota(jnp.int32, (8, 128), 1)
    gate = lane & 15
    gate_shift = shift & 15
    near_row, near_gate = lane >= shift - gate_shift, gate >= gate_shift
    f = [frame_ref[base + step] for step in (0, 1, UNITS, UNITS + 1)]
    z = jnp.where(
        near_row, jnp.where(near_gate, f[0], f[1]), jnp.where(near_gate, f[2], f[3])
    )
    return jnp.where(
        gate < 16 - gate_shift,
        pltpu.roll(z, (128 - shift) & 127, 1),
        pltpu.roll(z, (144 - shift) & 127, 1),
    )


PAIRS = 4
EARLY = 4
STEP = 3


def tiles_kernel(
    echo_hbm,
    weights_hbm,
    replica_hbm,
    dft_hbm,
    twist_hbm,
    doppler_hbm,
    gate_hbm,
    owner_hbm,
    tiles_ref,
    echo_ref,
    weights_ref,
    replica_ref,
    dft_ref,
    twist_ref,
    track_ref,
    code_ref,
    codes_ref,
    weight_ref,
    frame_ref,
    out_tile,
    out_strip,
    in_strip,
    all_weights,
    wide_ref,
    z_ref,
    acc_ref,
    out_block,
    y_ref,
    taps_ref,
    sum_ref,
    strip_sent,
    strip_here,
    strip_own,
    weight_sent,
    weight_here,
    block_sent,
    block_here,
    halo_sent,
    halo_here,
    edge_sent,
    edge_here,
    echo_loaded,
    loaded,
    code_moved,
    tile_sent,
    tile_here,
    row_here,
):
    me, g = lax.axis_index("pulse"), lax.axis_index("gate")
    gates = lax.axis_size("gate")
    barrier = pltpu.get_barrier_semaphore()

    def at(pulse, gate):
        return dict(device_id=(pulse, gate), device_id_type=pl.DeviceIdType.MESH)

    def peer(k):
        return lax.rem(me + k, 8)

    def load(pair):
        channels = pl.ds(pair * 2, 2)
        return pltpu.make_async_copy(
            echo_hbm.at[:, channels], echo_ref.at[:, channels], echo_loaded.at[pair]
        )

    small = [
        (weights_hbm, weights_ref),
        (replica_hbm, replica_ref),
        (dft_hbm, dft_ref),
        (twist_hbm, twist_ref),
        (doppler_hbm, track_ref.at[0]),
        (gate_hbm, track_ref.at[1]),
        (owner_hbm, track_ref.at[2]),
    ]
    loads = [
        pltpu.make_async_copy(source, target, loaded.at[k])
        for k, (source, target) in enumerate(small)
    ]
    for k in range(1, 8):
        pl.semaphore_signal(barrier, inc=1, **at(peer(k), g))
    for k in range(1, gates):
        pl.semaphore_signal(barrier, inc=1, **at(me, lax.rem(g + k, gates)))
    for pair in range(PAIRS):
        load(pair).start()
    for copy in loads:
        copy.start()

    def strip(unit, pair, target, source):
        return pltpu.make_async_remote_copy(
            src_ref=out_strip.at[unit, pair, target],
            dst_ref=in_strip.at[unit, pair, source],
            send_sem=strip_sent.at[unit, pair, target],
            recv_sem=strip_here.at[unit, pair, source],
            **at(target, g),
        )

    def own_strip(unit, pair):
        return pltpu.make_async_copy(
            out_strip.at[unit, pair, me], in_strip.at[unit, pair, me], strip_own.at[unit, pair]
        )

    def weight(target, source):
        return pltpu.make_async_remote_copy(
            src_ref=weight_ref,
            dst_ref=all_weights.at[source],
            send_sem=weight_sent.at[target],
            recv_sem=weight_here.at[source],
            **at(target, g),
        )

    def block(u, target, source):
        return pltpu.make_async_remote_copy(
            src_ref=out_block.at[u, target],
            dst_ref=y_ref.at[1 - u, source + u],
            send_sem=block_sent.at[u, target],
            recv_sem=block_here.at[u, source],
            **at(target, g),
        )

    def halo(u, source):
        return pltpu.make_async_remote_copy(
            src_ref=y_ref.at[1 - u, source + u],
            dst_ref=y_ref.at[1 - u, source + u + 8],
            send_sem=halo_sent.at[u, source],
            recv_sem=halo_here.at[u, source],
            **at(me, g - 1),
        )

    def edge(u):
        return pltpu.make_async_remote_copy(
            src_ref=y_ref.at[1 - u, (0, 8)[u]],
            dst_ref=y_ref.at[1 - u, (16, 0)[u]],
            send_sem=edge_sent.at[u],
            recv_sem=edge_here.at[u],
            **at(me, (g - 2, g + 1)[u]),
        )

    def turn(pair):
        load(pair).wait()
        for c in range(2):
            for q in range(2):
                turned = echo_ref[q, pair * 2 + c].T.reshape(8, 2, 16, 256)
                for unit in range(2):
                    out_strip[unit, pair, :, q, c] = turned[:, unit]

    def send(unit, pair):
        for k in range(1, 8):
            strip(unit, pair, peer(k), me).start()
        own_strip(unit, pair).start()

    loads[0].wait()
    for half in range(2):
        weight_ref[half] = weights_ref[:, 128 * half : 128 * half + 128]
    turn(0)
    pl.semaphore_wait(barrier, 7 + gates - 1)
    for k in range(1, 8):
        weight(peer(k), me).start()
    send(0, 0)
    for k in range(1, 8):
        pl.semaphore_signal(row_here, inc=1, **at(peer(k), g))

    def turn_and_send(pair, carry):
        turn(pair)
        send(0, pair)
        return carry

    def send_second(pair, carry):
        send(1, pair)
        return carry

    lax.fori_loop(1, PAIRS, turn_and_send, 0)
    lax.fori_loop(0, EARLY, send_second, 0)

    for copy in loads[1:]:
        copy.wait()
    code_ref[...] = slot_codes(track_ref[0], track_ref[1], track_ref[2], code_ref.shape[1])
    move = pltpu.make_async_copy(code_ref, codes_ref, code_moved)
    move.start()
    all_weights[me] = weight_ref[...]
    nothing = jnp.zeros((2 * ROWS, 256), BF16)

    @pl.when(g == 0)
    def _():
        y_ref[0, 0] = nothing

    @pl.when(g == gates - 1)
    def _():
        for k in range(8):
            y_ref[1, 8 + k] = nothing
            y_ref[0, 9 + k] = nothing

    @pl.when(g >= gates - 2)
    def _():
        y_ref[1, 16] = nothing

    make_taps(replica_ref, taps_ref)
    for k in range(1, 8):
        weight(me, peer(k)).wait_recv()

    def widen_step(i, carry):
        widen(i, all_weights, wide_ref)
        return carry

    lax.fori_loop(0, 32, widen_step, 0)
    move.wait()

    def transform(u, first, last):
        def one(pair, carry):
            own_strip(u, pair).wait()
            for k in range(1, 8):
                strip(u, pair, me, peer(k)).wait_recv()
            doppler_pair(
                pair, in_strip.at[u, pair], wide_ref, dft_ref, twist_ref, z_ref, acc_ref
            )
            return carry

        lax.fori_loop(first, last, one, 0)

    def send_blocks(u):
        for j in range(8):

            @pl.when(me == j)
            def _():
                pack_block(j, acc_ref, y_ref.at[1 - u, j + u])

            @pl.when(me != j)
            def _():
                pack_block(j, acc_ref, out_block.at[u, j])
                block(u, j, me).start()

    def pass_on(u, source):
        @pl.when(g > 0)
        def _():
            halo(u, source).start()

        if u == 0:

            @pl.when((source == 0) & (g > 1))
            def _():
                edge(0).start()

        else:

            @pl.when((source == 7) & (g < gates - 1))
            def _():
                edge(1).start()

    def pass_all(u):
        pass_on(u, me)

        def arrive(k, carry):
            source = peer(k)
            block(u, me, source).wait_recv()
            pass_on(u, source)
            return carry

        lax.fori_loop(1, 8, arrive, 0)

    def compress_unit(u):
        @pl.when(g < gates - 1)
        def _():
            for source in range(8):
                halo(u, source).wait_recv()

        @pl.when((g < gates - 2, g > 0)[u])
        def _():
            edge(u).wait_recv()

        compress(1 - u, y_ref, taps_ref, sum_ref)

    acc_ref[...] = jnp.zeros_like(acc_ref)
    transform(0, 0, PAIRS)
    send_blocks(0)
    acc_ref[...] = jnp.zeros_like(acc_ref)
    transform(1, 0, PAIRS)
    send_blocks(1)
    pass_all(0)
    pass_all(1)
    compress_unit(0)
    compress_unit(1)
    frame(g == 0, sum_ref, frame_ref.reshape(33 * UNITS * 8, 128))

    pl.semaphore_wait(row_here, 7)
    devices = 8 * gates
    here = me * gates + g

    def cut_block(owner):
        tiles = []
        for slot in range(5):
            code = codes_ref[0, owner * 5 + slot]
            base = jnp.clip(lax.shift_right_logical(code, 8), 0, 32 * UNITS - 2)
            tile = cut(base, code & 127, frame_ref)
            tiles.append(jnp.where(code & 128 != 0, tile, 0.0))
        return jnp.concatenate(tiles, axis=0).astype(BF16)

    def tile(owner, holder):
        return pltpu.make_async_remote_copy(
            src_ref=out_tile.at[owner],
            dst_ref=tiles_ref.at[holder],
            send_sem=tile_sent,
            recv_sem=tile_here,
            **at(owner // gates, lax.rem(owner, gates)),
        )

    def turned(k):
        return lax.rem(me + k // gates, 8) * gates + lax.rem(g + k, gates)

    def cut_and_send(step, carry):
        near = [turned(1 + step * STEP + k) for k in range(STEP)]
        for owner, part in zip(near, [cut_block(owner) for owner in near]):
            out_tile[owner] = part
        for owner in near:
            tile(owner, here).start()
        return carry

    steps = (devices - 1) // STEP
    lax.fori_loop(0, steps, cut_and_send, 0)
    for k in range(1 + steps * STEP, devices):
        owner = turned(k)
        out_tile[owner] = cut_block(owner)
        tile(owner, here).start()
    tiles_ref[here] = cut_block(here)

    for u in range(2):

        @pl.when(g > 0)
        def _():
            for source in range(8):
                halo(u, source).wait_send()

        @pl.when((g > 1, g < gates - 1)[u])
        def _():
            edge(u).wait_send()

    for k in range(1, 8):
        weight(peer(k), me).wait_send()
        for u in range(2):
            block(u, peer(k), me).wait_send()

    def sent(pair, carry):
        for k in range(1, 8):
            for u in range(2):
                strip(u, pair, peer(k), me).wait_send()
        return carry

    lax.fori_loop(0, PAIRS, sent, 0)
    everyone = pltpu.make_async_remote_copy(
        src_ref=out_tile.at[pl.ds(0, devices - 1)],
        dst_ref=tiles_ref.at[pl.ds(0, devices - 1)],
        send_sem=tile_sent,
        recv_sem=tile_here,
        **at(me, g),
    )
    everyone.wait_recv()
    everyone.wait_send()


def tiles(echoes, weights, replica, doppler, gate, owner, owners):
    dft, twist = tables()
    dma = pltpu.SemaphoreType.DMA
    hbm = pl.BlockSpec(memory_space=pltpu.HBM)
    return pl.pallas_call(
        tiles_kernel,
        out_shape=jax.ShapeDtypeStruct((owners, ROWS, 128), BF16),
        in_specs=[hbm] * 8,
        out_specs=VMEM,
        scratch_shapes=[
            pltpu.VMEM((2, 8, 256, 256), BF16),
            pltpu.VMEM((32, 256), F32),
            pltpu.VMEM((2, 256), BF16),
            pltpu.VMEM((512, 512), BF16),
            pltpu.VMEM((2, 8, 256), F32),
            pltpu.VMEM((3, 1, 256), jnp.int32),
            pltpu.VMEM((1, owners * 5), jnp.int32),
            pltpu.SMEM((1, owners * 5), jnp.int32),
            pltpu.VMEM((2, 32, 128), F32),
            pltpu.VMEM((33 * UNITS, 8, 128), F32),
            pltpu.VMEM((owners, ROWS, 128), BF16),
            pltpu.VMEM((2, PAIRS, 8, 2, 2, 16, 256), BF16),
            pltpu.VMEM((2, PAIRS, 8, 2, 2, 16, 256), BF16),
            pltpu.VMEM((8, 2, 32, 128), F32),
            pltpu.VMEM((32, 256, 128), F32),
            pltpu.VMEM((256, 512), BF16),
            pltpu.VMEM((2, 2, 272, 128), F32),
            pltpu.VMEM((2, 8, 2 * ROWS, 256), BF16),
            pltpu.VMEM((2, 17, 2 * ROWS, 256), BF16),
            pltpu.VMEM((17, 256, 256), BF16),
            pltpu.VMEM((2, UNITS * ROWS, 256), F32),
            dma((2, PAIRS, 8)),
            dma((2, PAIRS, 8)),
            dma((2, PAIRS)),
            dma((8,)),
            dma((8,)),
            dma((2, 8)),
            dma((2, 8)),
            dma((2, 8)),
            dma((2, 8)),
            dma((2,)),
            dma((2,)),
            dma((PAIRS,)),
            dma((7,)),
            dma(()),
            dma(()),
            dma(()),
            pltpu.SemaphoreType.REGULAR,
        ],
        compiler_params=params(60, collective_id=0, has_side_effects=True),
        cost_estimate=pl.CostEstimate(flops=6 * 10**9, bytes_accessed=8 << 20, transcendentals=0),
    )(echoes, weights, replica, jnp.asarray(dft), jnp.asarray(twist), doppler, gate, owner)


PARTS = 4


def rows_kernel(tiles_hbm, out_hbm, tiles_ref, wide_ref, out_ref, here, gone):
    holders, slots = tiles_ref.shape[1], out_ref.shape[1]
    loads = [
        pltpu.make_async_copy(
            tiles_hbm.at[pl.ds(part * holders, holders)], tiles_ref.at[part], here.at[part]
        )
        for part in range(PARTS)
    ]
    stores = [
        pltpu.make_async_copy(
            out_ref.at[part], out_hbm.at[pl.ds(part * slots, slots)], gone.at[part]
        )
        for part in range(PARTS)
    ]
    for load in loads:
        load.start()
    for part in range(PARTS):
        loads[part].wait()
        wide_ref[part] = tiles_ref[part].reshape(8 * slots, 128).astype(F32)
        for k in range(8):
            rows = wide_ref[part, pl.ds(k, slots, stride=8), :]
            out_ref[part, :, 128 * k : 128 * k + 128] = rows
        stores[part].start()
    for store in stores:
        store.wait()


def params(mib, **more):
    return pltpu.CompilerParams(vmem_limit_bytes=mib << 20, **more)


def local(echoes, replica, beam_weights, track_doppler, track_gate, track_owner):
    pulse_devices, gate_devices = lax.axis_size("pulse"), lax.axis_size("gate")
    owners = pulse_devices * gate_devices
    tracks = track_owner.shape[0]
    capacity = 5
    rows = (x.reshape(1, tracks) for x in (track_doppler, track_gate, track_owner))
    received = tiles(echoes, beam_weights.reshape(32, 256), replica, *rows, owners)
    hbm = pl.BlockSpec(memory_space=pltpu.HBM)
    slots = owners * capacity // PARTS
    return pl.pallas_call(
        rows_kernel,
        out_shape=jax.ShapeDtypeStruct((owners * capacity, 1024), F32),
        in_specs=[hbm],
        out_specs=hbm,
        scratch_shapes=[
            pltpu.VMEM((PARTS, owners // PARTS, capacity * 8, 128), BF16),
            pltpu.VMEM((PARTS, slots * 8, 128), F32),
            pltpu.VMEM((PARTS, slots, 1024), F32),
            pltpu.SemaphoreType.DMA((PARTS,)),
            pltpu.SemaphoreType.DMA((PARTS,)),
        ],
        compiler_params=params(60),
    )(received)


def solution(mesh):
    return jax.shard_map(
        local,
        mesh=mesh,
        in_specs=(
            P(None, None, "pulse", "gate"),
            P(),
            P(None, None, None, "pulse"),
            P(("pulse", "gate")),
            P(("pulse", "gate")),
            P(("pulse", "gate")),
        ),
        out_specs=P(("pulse", "gate"), None),
        check_vma=False,
    )
```

```python
import functools
import math

import jax
import jax.numpy as jnp
import numpy as np
from jax import lax
from jax.experimental import pallas as pl
from jax.experimental.pallas import tpu as pltpu
from jax.sharding import PartitionSpec as P

F32 = jnp.float32
BF16 = jnp.bfloat16
UNITS = 18
ROWS = 40
VMEM = pl.BlockSpec(memory_space=pltpu.VMEM)
SMEM = pl.BlockSpec(memory_space=pltpu.SMEM)


def tables():
    angle = 2.0 * np.pi * ((np.arange(256)[:, None] * np.arange(256)[None, :]) % 256) / 256.0
    cos, sin = np.cos(angle), np.sin(angle)
    dft = np.block([[cos, sin], [-sin, cos]]).astype(jnp.bfloat16)
    twist = 2.0 * np.pi * (np.arange(8)[:, None] * np.arange(256)[None, :]) / 2048.0
    scale = 1.0 / 1024.0
    return dft, np.stack([np.cos(twist) * scale, np.sin(twist) * scale]).astype(np.float32)


def cadd(a, b):
    return (a[0] + b[0], a[1] + b[1])


def csub(a, b):
    return (a[0] - b[0], a[1] - b[1])


def turn(a):
    return (a[1], -a[0])


def dft4(a):
    e0, e1 = cadd(a[0], a[2]), csub(a[0], a[2])
    f0, f1 = cadd(a[1], a[3]), turn(csub(a[1], a[3]))
    return [cadd(e0, f0), cadd(e1, f1), csub(e0, f0), csub(e1, f1)]


def dft8(x):
    root = math.sqrt(0.5)
    even = dft4([cadd(x[k], x[k + 4]) for k in range(4)])
    b = [csub(x[k], x[k + 4]) for k in range(4)]
    b1 = ((b[1][0] + b[1][1]) * root, (b[1][1] - b[1][0]) * root)
    b3 = ((b[3][1] - b[3][0]) * root, (b[3][0] + b[3][1]) * -root)
    odd = dft4([b[0], b1, turn(b[2]), b3])
    return [(even, odd)[d % 2][d // 2] for d in range(8)]


def doppler_pair(pair, x_ref, wide_ref, dft_ref, twist_ref, z_ref, acc_ref):
    for c in range(2):
        for half in range(2):
            cols = slice(128 * half, 128 * half + 128)
            x = [tuple(x_ref[pb, q, c, :, cols].astype(F32) for q in range(2)) for pb in range(8)]
            for d, (re, im) in enumerate(dft8(x)):
                cos, sin = (twist_ref[k, d : d + 1, cols] for k in range(2))
                at = slice(128 * c + 16 * d, 128 * c + 16 * d + 16)
                z_ref[at, 128 * half : 128 * half + 128] = (re * cos + im * sin).astype(BF16)
                z_ref[at, 256 + 128 * half : 384 + 128 * half] = (im * cos - re * sin).astype(BF16)
    spec = lax.dot_general(
        dft_ref[...], z_ref[...], (((1,), (1,)), ((), ())), preferred_element_type=F32
    )
    for b in range(2):
        real, imag = 0.0, 0.0
        for c in range(2):
            w_re, w_im = (wide_ref[(q * 2 + b) * 8 + 2 * pair + c] for q in range(2))
            cols = slice(128 * c, 128 * c + 128)
            re, im = spec[:256, cols], spec[256:, cols]
            real += w_re * re - w_im * im
            imag += w_re * im + w_im * re
        acc_ref[0, b, 8:264] += real
        acc_ref[1, b, 8:264] += imag


def widen(i, weight_ref, wide_ref):
    lane = lax.broadcasted_iota(jnp.int32, (16, 128), 1)
    keep = lane // 8 == lax.broadcasted_iota(jnp.int32, (16, 128), 0)
    spread = (
        lax.broadcasted_iota(jnp.int32, (128, 128), 0) % 8
        == lax.broadcasted_iota(jnp.int32, (128, 128), 1) // 16
    )
    spread = jnp.where(spread, 1.0, 0.0).astype(BF16)
    w = jnp.concatenate(
        [
            jnp.where(keep, weight_ref[source, half, pl.ds(i, 1), :], 0.0)
            for source in range(8)
            for half in range(2)
        ],
        axis=0,
    )
    wide_ref[i] = jnp.dot(w.astype(BF16), spread, preferred_element_type=F32)


def pack_block(j, acc_ref, out_ref):
    for q in range(2):
        both = jnp.concatenate(
            [acc_ref[q, b, 32 * j + 7 : 32 * j + 7 + ROWS] for b in range(2)], axis=0
        )
        out_ref[:, 128 * q : 128 * q + 128] = both.astype(BF16)


def make_taps(replica_ref, taps_ref):
    period = (
        lax.broadcasted_iota(jnp.int32, (16, 128), 0)
        == lax.broadcasted_iota(jnp.int32, (16, 128), 1) % 16
    )
    period = jnp.where(period, 1.0, 0.0).astype(F32)
    tables = []
    for q in range(2):
        row = jnp.concatenate(
            [replica_ref[q : q + 1, :].astype(F32), jnp.zeros((1, 128), F32)], axis=1
        )
        shifted = pltpu.roll(jnp.broadcast_to(row, (16, 384)), 0, 1, stride=1, stride_axis=0)
        tables.append(
            lax.dot_general(
                shifted.astype(BF16),
                period.astype(BF16),
                (((0,), (0,)), ((), ())),
                preferred_element_type=F32,
            )
        )
    lane = lax.broadcasted_iota(jnp.int32, (16, 128), 1) // 16
    for j in range(17):
        real, imag = (t[16 * j : 16 * j + 16] for t in tables)
        for d in range(8):
            keep = lane == d
            re, im = jnp.where(keep, real, 0.0), jnp.where(keep, imag, 0.0)
            from_real = jnp.concatenate([re, -im], axis=1).astype(BF16)
            from_imag = jnp.concatenate([im, re], axis=1).astype(BF16)
            taps_ref[j, 16 * d : 16 * d + 16, :] = from_real
            taps_ref[j, 128 + 16 * d : 144 + 16 * d, :] = from_imag


def compress(parity, y_ref, taps_ref, sum_ref):
    half, depth = UNITS // 2, 2 * ROWS
    for out in range(2):
        odd = (parity - out) % 2
        skip = out * (1 - parity)
        total = 9 - odd

        def part(first, count):
            x = jnp.concatenate(
                [
                    y_ref[parity, pl.ds(skip + first + k, half)].reshape(half * depth, 256)
                    for k in range(count)
                ],
                axis=1,
            )
            w = jnp.concatenate([taps_ref[odd + 2 * (first + k)] for k in range(count)], axis=0)
            return jnp.dot(x, w, preferred_element_type=F32)

        for first in range(0, 8, 4):
            count = 5 if first == 4 and total == 9 else 4
            if parity == 1 and first == 0:
                sum_ref[out] = part(first, count)
            else:
                sum_ref[out] += part(first, count)


def frame(first_block, sum_ref, frame_ref):
    for unit in range(UNITS):
        for q in range(2):
            for b in range(2):
                for half in range(2):
                    start = (unit // 2 * 2 + b) * ROWS + half
                    value = sum_ref[unit % 2, start : start + 33, 128 * q : 128 * q + 128]
                    if unit == 0:
                        value = jnp.where(first_block, 0.0, value)
                    at = pl.ds(unit * 8 + q * 4 + b * 2 + half, 33, stride=8 * UNITS)
                    frame_ref[at, :] = value


def slot_codes(doppler, gate, owner, slots):
    row, col = doppler & 255, (gate & 255) + 8
    base = lax.shift_right_logical(row, 3) * UNITS + lax.shift_right_logical(col, 4)
    code = (base * 256 + 128 + (row & 7) * 16 + (col & 15)).astype(F32)
    owner = owner.astype(F32)
    tracks = owner.shape[1]
    column = jnp.broadcast_to(owner, (8, tracks)).T[:, :1]
    square = (tracks, tracks)
    before = lax.broadcasted_iota(jnp.int32, square, 0) < lax.broadcasted_iota(jnp.int32, square, 1)
    same = jnp.where((column == owner) & before, 1.0, 0.0)
    slot = owner * 5.0 + jnp.sum(same, axis=0, keepdims=True)
    both = jnp.concatenate([slot, code, jnp.zeros((6, tracks), F32)], axis=0).T
    place = lax.broadcasted_iota(jnp.int32, (tracks, slots), 1).astype(F32)
    found = jnp.where(both[:, :1] == place, both[:, 1:2], 0.0)
    return jnp.sum(found, axis=0, keepdims=True).astype(jnp.int32)


def cut(base, shift, frame_ref):
    lane = lax.broadcasted_iota(jnp.int32, (8, 128), 1)
    gate = lane & 15
    gate_shift = shift & 15
    near_row, near_gate = lane >= shift - gate_shift, gate >= gate_shift
    f = [frame_ref[base + step] for step in (0, 1, UNITS, UNITS + 1)]
    z = jnp.where(
        near_row, jnp.where(near_gate, f[0], f[1]), jnp.where(near_gate, f[2], f[3])
    )
    return jnp.where(
        gate < 16 - gate_shift,
        pltpu.roll(z, (128 - shift) & 127, 1),
        pltpu.roll(z, (144 - shift) & 127, 1),
    )


PAIRS = 4
EARLY = 4
STEP = 3


def tiles_kernel(
    echo_hbm,
    weights_hbm,
    replica_hbm,
    dft_hbm,
    twist_hbm,
    doppler_hbm,
    gate_hbm,
    owner_hbm,
    tiles_ref,
    echo_ref,
    weights_ref,
    replica_ref,
    dft_ref,
    twist_ref,
    track_ref,
    code_ref,
    codes_ref,
    weight_ref,
    frame_ref,
    out_tile,
    out_strip,
    in_strip,
    all_weights,
    float_weights,
    wide_ref,
    z_ref,
    acc_ref,
    out_block,
    y_ref,
    taps_ref,
    sum_ref,
    strip_sent,
    strip_here,
    strip_own,
    weight_sent,
    weight_here,
    block_sent,
    block_here,
    halo_sent,
    halo_here,
    edge_sent,
    edge_here,
    echo_loaded,
    loaded,
    code_moved,
    tile_sent,
    tile_here,
    row_here,
):
    me, g = lax.axis_index("pulse"), lax.axis_index("gate")
    gates = lax.axis_size("gate")
    barrier = pltpu.get_barrier_semaphore()

    def at(pulse, gate):
        return dict(device_id=(pulse, gate), device_id_type=pl.DeviceIdType.MESH)

    def peer(k):
        return lax.rem(me + k, 8)

    def load(pair):
        channels = pl.ds(pair * 2, 2)
        return pltpu.make_async_copy(
            echo_hbm.at[:, channels], echo_ref.at[:, channels], echo_loaded.at[pair]
        )

    small = [
        (weights_hbm, weights_ref),
        (replica_hbm, replica_ref),
        (dft_hbm, dft_ref),
        (twist_hbm, twist_ref),
        (doppler_hbm, track_ref.at[0]),
        (gate_hbm, track_ref.at[1]),
        (owner_hbm, track_ref.at[2]),
    ]
    loads = [
        pltpu.make_async_copy(source, target, loaded.at[k])
        for k, (source, target) in enumerate(small)
    ]
    for k in range(1, 8):
        pl.semaphore_signal(barrier, inc=1, **at(peer(k), g))
    for k in range(1, gates):
        pl.semaphore_signal(barrier, inc=1, **at(me, lax.rem(g + k, gates)))
    for pair in range(PAIRS):
        load(pair).start()
    for copy in loads:
        copy.start()

    def strip(unit, pair, target, source):
        return pltpu.make_async_remote_copy(
            src_ref=out_strip.at[unit, pair, target],
            dst_ref=in_strip.at[unit, pair, source],
            send_sem=strip_sent.at[unit, pair, target],
            recv_sem=strip_here.at[unit, pair, source],
            **at(target, g),
        )

    def own_strip(unit, pair):
        return pltpu.make_async_copy(
            out_strip.at[unit, pair, me], in_strip.at[unit, pair, me], strip_own.at[unit, pair]
        )

    def weight(target, source):
        return pltpu.make_async_remote_copy(
            src_ref=weight_ref,
            dst_ref=all_weights.at[source],
            send_sem=weight_sent.at[target],
            recv_sem=weight_here.at[source],
            **at(target, g),
        )

    def block(u, target, source):
        return pltpu.make_async_remote_copy(
            src_ref=out_block.at[u, target],
            dst_ref=y_ref.at[1 - u, source + u],
            send_sem=block_sent.at[u, target],
            recv_sem=block_here.at[u, source],
            **at(target, g),
        )

    def halo(u, source):
        return pltpu.make_async_remote_copy(
            src_ref=y_ref.at[1 - u, source + u],
            dst_ref=y_ref.at[1 - u, source + u + 8],
            send_sem=halo_sent.at[u, source],
            recv_sem=halo_here.at[u, source],
            **at(me, g - 1),
        )

    def edge(u):
        return pltpu.make_async_remote_copy(
            src_ref=y_ref.at[1 - u, (0, 8)[u]],
            dst_ref=y_ref.at[1 - u, (16, 0)[u]],
            send_sem=edge_sent.at[u],
            recv_sem=edge_here.at[u],
            **at(me, (g - 2, g + 1)[u]),
        )

    def turn(pair):
        load(pair).wait()
        for c in range(2):
            for q in range(2):
                turned = echo_ref[q, pair * 2 + c].T.reshape(8, 2, 16, 256)
                for unit in range(2):
                    out_strip[unit, pair, :, q, c] = turned[:, unit]

    def send(unit, pair):
        for k in range(1, 8):
            strip(unit, pair, peer(k), me).start()
        own_strip(unit, pair).start()

    loads[0].wait()
    for half in range(2):
        weight_ref[half] = weights_ref[:, 128 * half : 128 * half + 128].astype(BF16)
    turn(0)
    pl.semaphore_wait(barrier, 7 + gates - 1)
    for k in range(1, 8):
        weight(peer(k), me).start()
    send(0, 0)
    for k in range(1, 8):
        pl.semaphore_signal(row_here, inc=1, **at(peer(k), g))

    def turn_and_send(pair, carry):
        turn(pair)
        send(0, pair)
        return carry

    def send_second(pair, carry):
        send(1, pair)
        return carry

    lax.fori_loop(1, PAIRS, turn_and_send, 0)
    lax.fori_loop(0, EARLY, send_second, 0)

    for copy in loads[1:]:
        copy.wait()
    code_ref[...] = slot_codes(track_ref[0], track_ref[1], track_ref[2], code_ref.shape[1])
    move = pltpu.make_async_copy(code_ref, codes_ref, code_moved)
    move.start()
    all_weights[me] = weight_ref[...]
    nothing = jnp.zeros((2 * ROWS, 256), BF16)

    @pl.when(g == 0)
    def _():
        y_ref[0, 0] = nothing

    @pl.when(g == gates - 1)
    def _():
        for k in range(8):
            y_ref[1, 8 + k] = nothing
            y_ref[0, 9 + k] = nothing

    @pl.when(g >= gates - 2)
    def _():
        y_ref[1, 16] = nothing

    make_taps(replica_ref, taps_ref)
    for k in range(1, 8):
        weight(me, peer(k)).wait_recv()
    float_weights[...] = all_weights[...].astype(F32)

    def widen_step(i, carry):
        widen(i, float_weights, wide_ref)
        return carry

    lax.fori_loop(0, 32, widen_step, 0)
    move.wait()

    def transform(u, first, last):
        def one(pair, carry):
            own_strip(u, pair).wait()
            for k in range(1, 8):
                strip(u, pair, me, peer(k)).wait_recv()
            doppler_pair(
                pair, in_strip.at[u, pair], wide_ref, dft_ref, twist_ref, z_ref, acc_ref
            )
            return carry

        lax.fori_loop(first, last, one, 0)

    def send_blocks(u):
        for j in range(8):

            @pl.when(me == j)
            def _():
                pack_block(j, acc_ref, y_ref.at[1 - u, j + u])

            @pl.when(me != j)
            def _():
                pack_block(j, acc_ref, out_block.at[u, j])
                block(u, j, me).start()

    def pass_on(u, source):
        @pl.when(g > 0)
        def _():
            halo(u, source).start()

        if u == 0:

            @pl.when((source == 0) & (g > 1))
            def _():
                edge(0).start()

        else:

            @pl.when((source == 7) & (g < gates - 1))
            def _():
                edge(1).start()

    def pass_all(u):
        pass_on(u, me)

        def arrive(k, carry):
            source = peer(k)
            block(u, me, source).wait_recv()
            pass_on(u, source)
            return carry

        lax.fori_loop(1, 8, arrive, 0)

    def compress_unit(u):
        @pl.when(g < gates - 1)
        def _():
            for source in range(8):
                halo(u, source).wait_recv()

        @pl.when((g < gates - 2, g > 0)[u])
        def _():
            edge(u).wait_recv()

        compress(1 - u, y_ref, taps_ref, sum_ref)

    acc_ref[...] = jnp.zeros_like(acc_ref)
    transform(0, 0, PAIRS)
    send_blocks(0)
    acc_ref[...] = jnp.zeros_like(acc_ref)
    transform(1, 0, PAIRS)
    send_blocks(1)
    pass_all(0)
    pass_all(1)
    compress_unit(0)
    compress_unit(1)
    frame(g == 0, sum_ref, frame_ref.reshape(33 * UNITS * 8, 128))

    pl.semaphore_wait(row_here, 7)
    devices = 8 * gates
    here = me * gates + g

    def cut_block(owner):
        tiles = []
        for slot in range(5):
            code = codes_ref[0, owner * 5 + slot]
            base = jnp.clip(lax.shift_right_logical(code, 8), 0, 32 * UNITS - 2)
            tile = cut(base, code & 127, frame_ref)
            tiles.append(jnp.where(code & 128 != 0, tile, 0.0))
        return jnp.concatenate(tiles, axis=0).astype(BF16)

    def tile(owner, holder):
        return pltpu.make_async_remote_copy(
            src_ref=out_tile.at[owner],
            dst_ref=tiles_ref.at[holder],
            send_sem=tile_sent,
            recv_sem=tile_here,
            **at(owner // gates, lax.rem(owner, gates)),
        )

    def turned(k):
        return lax.rem(me + k // gates, 8) * gates + lax.rem(g + 5 * k, gates)

    def cut_and_send(step, carry):
        near = [turned(1 + step * STEP + k) for k in range(STEP)]
        for owner, part in zip(near, [cut_block(owner) for owner in near]):
            out_tile[owner] = part
        for owner in near:
            tile(owner, here).start()
        return carry

    steps = (devices - 1) // STEP
    lax.fori_loop(0, steps, cut_and_send, 0)
    for k in range(1 + steps * STEP, devices):
        owner = turned(k)
        out_tile[owner] = cut_block(owner)
        tile(owner, here).start()
    tiles_ref[here] = cut_block(here)

    for u in range(2):

        @pl.when(g > 0)
        def _():
            for source in range(8):
                halo(u, source).wait_send()

        @pl.when((g > 1, g < gates - 1)[u])
        def _():
            edge(u).wait_send()

    for k in range(1, 8):
        weight(peer(k), me).wait_send()
        for u in range(2):
            block(u, peer(k), me).wait_send()

    def sent(pair, carry):
        for k in range(1, 8):
            for u in range(2):
                strip(u, pair, peer(k), me).wait_send()
        return carry

    lax.fori_loop(0, PAIRS, sent, 0)
    everyone = pltpu.make_async_remote_copy(
        src_ref=out_tile.at[pl.ds(0, devices - 1)],
        dst_ref=tiles_ref.at[pl.ds(0, devices - 1)],
        send_sem=tile_sent,
        recv_sem=tile_here,
        **at(me, g),
    )
    everyone.wait_recv()
    everyone.wait_send()


def tiles(echoes, weights, replica, doppler, gate, owner, owners):
    dft, twist = tables()
    dma = pltpu.SemaphoreType.DMA
    hbm = pl.BlockSpec(memory_space=pltpu.HBM)
    return pl.pallas_call(
        tiles_kernel,
        out_shape=jax.ShapeDtypeStruct((owners, ROWS, 128), BF16),
        in_specs=[hbm] * 8,
        out_specs=VMEM,
        scratch_shapes=[
            pltpu.VMEM((2, 8, 256, 256), BF16),
            pltpu.VMEM((32, 256), F32),
            pltpu.VMEM((2, 256), BF16),
            pltpu.VMEM((512, 512), BF16),
            pltpu.VMEM((2, 8, 256), F32),
            pltpu.VMEM((3, 1, 256), jnp.int32),
            pltpu.VMEM((1, owners * 5), jnp.int32),
            pltpu.SMEM((1, owners * 5), jnp.int32),
            pltpu.VMEM((2, 32, 128), BF16),
            pltpu.VMEM((33 * UNITS, 8, 128), F32),
            pltpu.VMEM((owners, ROWS, 128), BF16),
            pltpu.VMEM((2, PAIRS, 8, 2, 2, 16, 256), BF16),
            pltpu.VMEM((2, PAIRS, 8, 2, 2, 16, 256), BF16),
            pltpu.VMEM((8, 2, 32, 128), BF16),
            pltpu.VMEM((8, 2, 32, 128), F32),
            pltpu.VMEM((32, 256, 128), F32),
            pltpu.VMEM((256, 512), BF16),
            pltpu.VMEM((2, 2, 272, 128), F32),
            pltpu.VMEM((2, 8, 2 * ROWS, 256), BF16),
            pltpu.VMEM((2, 17, 2 * ROWS, 256), BF16),
            pltpu.VMEM((17, 256, 256), BF16),
            pltpu.VMEM((2, UNITS * ROWS, 256), F32),
            dma((2, PAIRS, 8)),
            dma((2, PAIRS, 8)),
            dma((2, PAIRS)),
            dma((8,)),
            dma((8,)),
            dma((2, 8)),
            dma((2, 8)),
            dma((2, 8)),
            dma((2, 8)),
            dma((2,)),
            dma((2,)),
            dma((PAIRS,)),
            dma((7,)),
            dma(()),
            dma(()),
            dma(()),
            pltpu.SemaphoreType.REGULAR,
        ],
        compiler_params=params(60, collective_id=0, has_side_effects=True),
        cost_estimate=pl.CostEstimate(flops=6 * 10**9, bytes_accessed=8 << 20, transcendentals=0),
    )(echoes, weights, replica, jnp.asarray(dft), jnp.asarray(twist), doppler, gate, owner)


PARTS = 4


def rows_kernel(tiles_hbm, out_hbm, tiles_ref, wide_ref, out_ref, here, gone):
    holders, slots = tiles_ref.shape[1], out_ref.shape[1]
    loads = [
        pltpu.make_async_copy(
            tiles_hbm.at[pl.ds(part * holders, holders)], tiles_ref.at[part], here.at[part]
        )
        for part in range(PARTS)
    ]
    stores = [
        pltpu.make_async_copy(
            out_ref.at[part], out_hbm.at[pl.ds(part * slots, slots)], gone.at[part]
        )
        for part in range(PARTS)
    ]
    for load in loads:
        load.start()
    for part in range(PARTS):
        loads[part].wait()
        wide_ref[part] = tiles_ref[part].reshape(8 * slots, 128).astype(F32)
        for k in range(8):
            rows = wide_ref[part, pl.ds(k, slots, stride=8), :]
            out_ref[part, :, 128 * k : 128 * k + 128] = rows
        stores[part].start()
    for store in stores:
        store.wait()


def params(mib, **more):
    return pltpu.CompilerParams(vmem_limit_bytes=mib << 20, **more)


def local(echoes, replica, beam_weights, track_doppler, track_gate, track_owner):
    pulse_devices, gate_devices = lax.axis_size("pulse"), lax.axis_size("gate")
    owners = pulse_devices * gate_devices
    tracks = track_owner.shape[0]
    capacity = 5
    rows = (x.reshape(1, tracks) for x in (track_doppler, track_gate, track_owner))
    received = tiles(echoes, beam_weights.reshape(32, 256), replica, *rows, owners)
    hbm = pl.BlockSpec(memory_space=pltpu.HBM)
    slots = owners * capacity // PARTS
    return pl.pallas_call(
        rows_kernel,
        out_shape=jax.ShapeDtypeStruct((owners * capacity, 1024), F32),
        in_specs=[hbm],
        out_specs=hbm,
        scratch_shapes=[
            pltpu.VMEM((PARTS, owners // PARTS, capacity * 8, 128), BF16),
            pltpu.VMEM((PARTS, slots * 8, 128), F32),
            pltpu.VMEM((PARTS, slots, 1024), F32),
            pltpu.SemaphoreType.DMA((PARTS,)),
            pltpu.SemaphoreType.DMA((PARTS,)),
        ],
        compiler_params=params(60),
    )(received)


def solution(mesh):
    return jax.shard_map(
        local,
        mesh=mesh,
        in_specs=(
            P(None, None, "pulse", "gate"),
            P(),
            P(None, None, None, "pulse"),
            P(("pulse", "gate")),
            P(("pulse", "gate")),
            P(("pulse", "gate")),
        ),
        out_specs=P(("pulse", "gate"), None),
        check_vma=False,
    )
```
